512 devices in a mesh: gx: 16 (over x, y), gy: 32 (over z, core).
Axes of the slice: x: 4, y: 4, z: 16, core: 2. Of those that a mesh axis runs over, the one named last changes fastest.
Arguments:
- vol_rhs: float32 [2, 120, 524288], P(None, None, ('gx', 'gy')), may hold values from -6 to 6
- trace_in: float32 [2, 36, 1048576], P(None, None, ('gx', 'gy')), may hold values from -6 to 6
- pml_flag: int32 [524288], P(('gx', 'gy')), may hold values 0 or 1
- stretch: float32 [524288], P(('gx', 'gy')), may hold values from 0.5 to 4
- cond_op: float32 [4, 2, 36, 120], replicated, may hold values from -0.375 to 0.375
- skel_op: float32 [7, 2, 36, 36], replicated, may hold values from -1 to 4
- block_coef: float32 [7, 2, 1048576], P(None, None, ('gx', 'gy')), may hold values from -27 to 27
- recon_op: float32 [2, 120, 120], replicated, may hold values from -0.375 to 0.375
- lift_op: float32 [4, 2, 120, 36], replicated, may hold values from -0.375 to 0.375
- elem_face: int32 [4, 524288], P(None, ('gx', 'gy')), may hold values from 0 to 4095, as said below
- adjacency: int32 [6, 1048576], P(None, ('gx', 'gy')), may hold values from -1 to 4095, as said below
- halo_list: int32 [8, 131072], P(None, ('gx', 'gy')), may hold values from -1 to 2047, as said below
Outputs:
- trace_out: float32 [2, 36, 1048576], P(None, None, ('gx', 'gy'))
- volume_out: float32 [2, 120, 524288], P(None, None, ('gx', 'gy'))
The draws below stay inside these ranges and needn't reach their ends.
Inputs may be any that keep to these rules, and one draw needn't show every extreme that they name: The list of direction d of partition p is halo_list[d, p * 256 .. (p + 1) * 256 - 1], local face numbers of p: its live entries are distinct and come first, -1 fills the rest; lists towards a position outside the grid are empty; in every draw some list is full. `elem_face`: every ghost slot named is a live entry of the list of an existing partition. `adjacency`: every ghost slot named is a live entry of the list of an existing partition; each face has 3 or 6 live entries, first, then -1.
All inputs are finite; a program needn't handle non-finite values. No bound on the sum of `pml_flag` on one device may be relied on, other than what follows from the above.
Results may differ from the reference program's by a relative error of at most 0.0003.
Values sent between devices are 32-bit elements; how exact they have to be, the bound alone decides.
No kernel may reach another device: no remote copies, remote signals or barrier semaphores. Data moves between devices by JAX's collectives and lax.ppermute only.
A program may use at most 128 MiB of HBM per device.

```python
import math
import jax
import jax.numpy as jnp
from jax import lax

NQ = 36
NV = 120
NADJ = 6
DIRS = 8
E_DEV = 1024
F_DEV = 2048
HALO = 256
ELEMS = 524288
FACES = 1048576
N_GX = 16
N_GY = 32
DEVICES = 512


OFFSETS = ((-1, -1), (-1, 0), (-1, 1), (0, -1), (0, 1), (1, -1), (1, 0), (1, 1))


def offset_tables():
    return (jnp.array([entry[0] for entry in OFFSETS], jnp.int32), jnp.array([entry[1] for entry in OFFSETS], jnp.int32))


def halo_counts(key):
    shift_x, shift_y = offset_tables()
    device = jnp.arange(DEVICES, dtype=jnp.int32)
    target_x = (device // N_GY)[:, None] + shift_x[None, :]
    target_y = (device % N_GY)[:, None] + shift_y[None, :]
    exists = (target_x >= 0) & (target_x < N_GX) & (target_y >= 0) & (target_y < N_GY)
    counts = jax.random.randint(jax.random.fold_in(key, 11), (DEVICES, DIRS), HALO // 4, HALO + 1)
    chosen = jax.random.randint(jax.random.fold_in(key, 12), (), 0, DEVICES)
    counts = jnp.where(device[:, None] == chosen, HALO, counts)
    return jnp.where(exists, counts, 0)


def draw_targets(key, salt, entries):
    counts = halo_counts(key)
    shift_x, shift_y = offset_tables()
    subkeys = jax.random.split(jax.random.fold_in(key, salt), 4)
    device = jnp.arange(DEVICES, dtype=jnp.int32)[:, None]
    local_pick = jax.random.randint(subkeys[0], (DEVICES, entries), 0, F_DEV)
    direction = jax.random.randint(subkeys[1], (DEVICES, entries), 0, DIRS)
    sender_x = device // N_GY - shift_x[direction]
    sender_y = device % N_GY - shift_y[direction]
    inside = (sender_x >= 0) & (sender_x < N_GX) & (sender_y >= 0) & (sender_y < N_GY)
    sender = jnp.clip(sender_x, 0, N_GX - 1) * N_GY + jnp.clip(sender_y, 0, N_GY - 1)
    available = jnp.where(inside, counts[sender, direction], 0)
    position = jax.random.randint(subkeys[2], (DEVICES, entries), 0, 1 << 20) % jnp.maximum(available, 1)
    use_ghost = (jax.random.randint(subkeys[3], (DEVICES, entries), 0, 10) < 3) & (available > 0)
    return jnp.where(use_ghost, F_DEV + direction * HALO + position, local_pick)


def draw_elem_face(key, part):
    targets = draw_targets(key, 21, 4 * E_DEV).reshape(DEVICES, 4, E_DEV)
    return targets.transpose(1, 0, 2).reshape(4, ELEMS).astype(jnp.int32)


def draw_adjacency(key, part):
    targets = draw_targets(key, 31, NADJ * F_DEV).reshape(DEVICES, NADJ, F_DEV)
    boundary_face = jax.random.randint(jax.random.fold_in(key, 32), (DEVICES, 1, F_DEV), 0, 5) == 0
    live_count = jnp.where(boundary_face, 3, NADJ)
    slot_rank = jnp.arange(NADJ, dtype=jnp.int32)[None, :, None]
    padded_targets = jnp.where(slot_rank < live_count, targets, -1)
    return padded_targets.transpose(1, 0, 2).reshape(NADJ, FACES).astype(jnp.int32)


def draw_prefix(subkey):
    return jax.random.permutation(subkey, F_DEV)[:HALO]


def draw_halo_list(key, part):
    counts = halo_counts(key)
    subkeys = jax.random.split(jax.random.fold_in(key, 13), DEVICES * DIRS)
    chosen_faces = jax.vmap(draw_prefix)(subkeys).reshape(DEVICES, DIRS, HALO)
    is_live = jnp.arange(HALO, dtype=jnp.int32)[None, None, :] < counts[:, :, None]
    halo_rows = jnp.where(is_live, chosen_faces, -1)
    return halo_rows.transpose(1, 0, 2).reshape(DIRS, DEVICES * HALO).astype(jnp.int32)


def draw_skel_op(key, part):
    noise = jnp.clip(jax.random.normal(key, (NADJ + 1, 2, NQ, NQ), jnp.float32), -4.0, 4.0)
    scaled = noise * NQ ** (-0.5)
    centre = 3.0 * jnp.eye(NQ, dtype=jnp.float32) + 0.25 * noise[0, 0]
    return scaled.at[0, 0].set(centre).at[0, 1].set(0.25 * noise[0, 1])


def draw_block_coef(key, part):
    subkeys = jax.random.split(key, 2)
    device = (jnp.arange(FACES, dtype=jnp.int32) // F_DEV).astype(jnp.float32)
    level = device / max(DEVICES - 1, 1)
    magnitude = jnp.exp(jax.random.uniform(subkeys[0], (NADJ + 1, FACES), jnp.float32, jnp.log(0.5), jnp.log(2.0)))
    rising = 3.0 ** level
    phase = jax.random.uniform(subkeys[1], (NADJ + 1, FACES), jnp.float32, -3.14159, 3.14159)
    phase = phase.at[0].multiply(0.15)
    size_all = magnitude * rising[None, :]
    return jnp.stack([size_all * jnp.cos(phase), size_all * jnp.sin(phase)], axis=1)


def with_ends(drawn, stream_key, low, high):
    place = [jax.random.randint(jax.random.fold_in(stream_key, axis), (), 0, length) for axis, length in enumerate(drawn.shape)]
    longest = drawn.shape.index(max(drawn.shape))
    beside = place[:longest] + [(place[longest] + 1) % drawn.shape[longest]] + place[longest + 1:]
    return drawn.at[tuple(place)].set(low).at[tuple(beside)].set(high)


def level_of(rng, dims, cuts, low, top_value):
    gain = 1.0
    for dim, blocks in cuts:
        steps = jax.random.uniform(jax.random.fold_in(jax.random.fold_in(rng, 6), dim), (blocks,), jnp.float32, low / len(cuts), top_value / len(cuts))
        gain = gain * jnp.repeat(jnp.exp(steps), dims[dim] // blocks).reshape((-1,) + (1,) * (len(dims) - 1 - dim))
    return gain


def gaussian(stream_key, dims, width, bound, shards=(), kind=jnp.bfloat16):
    values = jax.random.normal(stream_key, dims, jnp.float32) * width
    if len(shards) > 0:
        values = level_of(stream_key, dims, shards, -0.22, 0.18) * values
    return jnp.clip(values, min=-bound, max=bound).astype(kind)


def setup_inputs(seed: int = 0) -> dict:
    splits = jax.random.split(jax.random.key(seed), 13)
    return {
        "vol_rhs": gaussian(splits[0], (2, NV, ELEMS), 1.0, 6.0, ((2, 512),), jnp.float32),
        "trace_in": gaussian(splits[1], (2, NQ, FACES), 1.0, 6.0, ((2, 512),), jnp.float32),
        "pml_flag": with_ends((jax.random.randint(splits[2], (ELEMS,), 0, 3) < 1).astype(jnp.int32), jax.random.fold_in(splits[2], 1), 0, 1),
        "stretch": jnp.clip(jnp.exp(math.log(4.0) - 2.0794415 * jax.random.uniform(splits[3], (ELEMS,), jnp.float32) ** level_of(splits[3], (ELEMS,), ((0, 512),), -0.2, 0.2)), 0.5, 4.0),
        "cond_op": gaussian(splits[4], (4, 2, NQ, NV), (2 * NV) ** -0.5, 0.375, (), jnp.float32),
        "skel_op": draw_skel_op(jax.random.fold_in(splits[12], 71), 0),
        "block_coef": draw_block_coef(jax.random.fold_in(splits[12], 71), 0),
        "recon_op": gaussian(splits[7], (2, NV, NV), (2 * NV) ** -0.5, 0.375, (), jnp.float32),
        "lift_op": gaussian(splits[8], (4, 2, NV, NQ), (8 * NQ) ** -0.5, 0.375, (), jnp.float32),
        "elem_face": draw_elem_face(jax.random.fold_in(splits[12], 71), 0),
        "adjacency": draw_adjacency(jax.random.fold_in(splits[12], 71), 0),
        "halo_list": draw_halo_list(jax.random.fold_in(splits[12], 71), 0),
    }


OFFSETS = ((-1, -1), (-1, 0), (-1, 1), (0, -1), (0, 1), (1, -1), (1, 0), (1, 1))


def complex_block(complex_pair):
    top_row = jnp.concatenate([complex_pair[0], -complex_pair[1]], axis=1)
    bottom_row = jnp.concatenate([complex_pair[1], complex_pair[0]], axis=1)
    return jnp.concatenate([top_row, bottom_row], axis=0)


def complex_scale(scale_real, scale_imag, vector):
    half_rows = vector.shape[-2] // 2
    real_part = vector[..., :half_rows, :]
    imag_part = vector[..., half_rows:, :]
    return jnp.concatenate([scale_real * real_part - scale_imag * imag_part, scale_real * imag_part + scale_imag * real_part], axis=-2)


def apply_matrix(matrix, batched):
    return jnp.einsum("ij,pjn->pin", matrix, batched, precision=lax.Precision.HIGHEST)


def take_columns(values, columns):
    clipped = jnp.maximum(columns, 0)
    picked = jax.vmap(lambda source, wanted: source[:, wanted])(values, clipped)
    return jnp.where(columns[:, None, :] >= 0, picked, 0.0)


def add_columns(target, columns, values):
    return target.at[:, columns].add(values)


def grid_shift(blocks, step_x, step_y):
    grid_view = blocks.reshape((N_GX, N_GY) + blocks.shape[1:])
    widths = ((1, 1), (1, 1)) + ((0, 0),) * (blocks.ndim - 1)
    padded = jnp.pad(grid_view, widths)
    moved = padded[1 - step_x:1 - step_x + N_GX, 1 - step_y:1 - step_y + N_GY]
    return moved.reshape(blocks.shape)


def per_device(array, rows):
    return array.reshape(rows, DEVICES, -1).transpose(1, 0, 2)


def to_global(batched, shape):
    return batched.transpose(1, 0, 2).reshape(shape)


def with_ghosts(own_faces, lists):
    outgoing = take_columns(own_faces, lists.reshape(DEVICES, DIRS * HALO))
    outgoing = outgoing.reshape(DEVICES, own_faces.shape[1], DIRS, HALO)
    arrived = [grid_shift(outgoing[:, :, direction], OFFSETS[direction][0], OFFSETS[direction][1]) for direction in range(DIRS)]
    return jnp.concatenate([own_faces] + arrived, axis=2)


def owner_sum(collected, lists):
    own_faces = collected[:, :, :F_DEV]
    for direction in range(DIRS):
        offset_at = F_DEV + direction * HALO
        returned = grid_shift(collected[:, :, offset_at:offset_at + HALO], -OFFSETS[direction][0], -OFFSETS[direction][1])
        columns = lists[:, direction]
        returned = jnp.where(columns[:, None, :] >= 0, returned, 0.0)
        own_faces = jax.vmap(add_columns)(own_faces, jnp.maximum(columns, 0), returned)
    return own_faces


def reference(vol_rhs, trace_in, pml_flag, stretch, cond_op, skel_op, block_coef, recon_op, lift_op, elem_face, adjacency, halo_list):
    trace_rows = 2 * NQ
    volume = per_device(vol_rhs, 2 * NV)
    traces = per_device(trace_in, trace_rows)
    pml_tilt = (pml_flag.astype(jnp.float32) * stretch).reshape(DEVICES, 1, E_DEV)
    lists = halo_list.reshape(DIRS, DEVICES, HALO).transpose(1, 0, 2)
    slots = elem_face.reshape(4, DEVICES, E_DEV).transpose(1, 0, 2).reshape(DEVICES, 4 * E_DEV)
    neighbours = adjacency.reshape(NADJ, DEVICES, F_DEV).transpose(1, 0, 2)
    coefficient = block_coef.reshape(NADJ + 1, 2, DEVICES, F_DEV).transpose(2, 0, 1, 3)
    cond_big = jnp.concatenate([complex_block(cond_op[corner]) for corner in range(4)], axis=0)
    pieces = apply_matrix(cond_big, volume).reshape(DEVICES, 4, trace_rows, E_DEV)
    pieces = complex_scale(1.0, pml_tilt[:, None], pieces)
    flat_pieces = pieces.transpose(0, 2, 1, 3).reshape(DEVICES, trace_rows, 4 * E_DEV)
    collected = jnp.zeros((DEVICES, trace_rows, F_DEV + DIRS * HALO), jnp.float32)
    collected = jax.vmap(add_columns)(collected, slots, flat_pieces)
    rhs_skeleton = owner_sum(collected, lists)
    skel_blocks = [complex_block(skel_op[block_number]) for block_number in range(NADJ + 1)]

    def skeleton(own_faces):
        extended = with_ghosts(own_faces, lists)
        result = complex_scale(coefficient[:, 0, 0:1], coefficient[:, 0, 1:2], apply_matrix(skel_blocks[0], own_faces))
        for neighbour in range(NADJ):
            gathered = take_columns(extended, neighbours[:, neighbour])
            product = apply_matrix(skel_blocks[neighbour + 1], gathered)
            result = result + complex_scale(coefficient[:, neighbour + 1, 0:1], coefficient[:, neighbour + 1, 1:2], product)
        return result

    residual_now = rhs_skeleton - skeleton(traces)
    image = skeleton(residual_now)
    image_real = image[:, :NQ]
    image_imag = image[:, NQ:]
    residual_real = residual_now[:, :NQ]
    residual_imag = residual_now[:, NQ:]
    numer_real = jnp.sum(image_real * residual_real + image_imag * residual_imag)
    numer_imag = jnp.sum(image_real * residual_imag - image_imag * residual_real)
    power_sum = jnp.sum(image * image)
    step_real = numer_real / power_sum
    step_imag = numer_imag / power_sum
    trace_new = traces + complex_scale(step_real, step_imag, residual_now)
    extended = with_ghosts(trace_new, lists)
    picked = take_columns(extended, slots).reshape(DEVICES, trace_rows, 4, E_DEV)
    picked = picked.transpose(0, 2, 1, 3).reshape(DEVICES, 4 * trace_rows, E_DEV)
    lift_big = jnp.concatenate([complex_block(lift_op[corner]) for corner in range(4)], axis=1)
    volume_new = complex_scale(1.0, pml_tilt, apply_matrix(complex_block(recon_op), volume)) - apply_matrix(lift_big, picked)
    return to_global(trace_new, (2, NQ, FACES)), to_global(volume_new, (2, NV, ELEMS))
```

```python
import functools

import jax
import jax.numpy as jnp
from jax import lax
from jax.experimental import pallas as pl
from jax.experimental.pallas import tpu as pltpu
from jax.sharding import PartitionSpec as P

F32 = jnp.float32
BF16 = jnp.bfloat16
HALF = 40
ROWS = 2 * HALF
LANES = 128
PAD = 8
DIRS = 8
UNROLL = 16
MIB = 1 << 20


def split(values):
    high = values.astype(BF16)
    return high, (values - high.astype(F32)).astype(BF16)


def dot(left, right, left_dim=1, right_dim=0):
    return lax.dot_general(
        left, right, (((left_dim,), (right_dim,)), ((), ())), preferred_element_type=F32
    )


def half_rolled(block, height):
    wide = jnp.concatenate(
        [block, jnp.zeros((height, LANES - block.shape[1]), F32)], axis=1
    )
    return wide, pltpu.roll(wide, HALF, 1)


def gather_rows(count, index_of, source, target, base=0):
    def some(step, carry):
        first = step * UNROLL
        for extra in range(UNROLL):
            row = index_of(first + extra)
            target[pl.ds(base + first + extra, 1), :] = source[pl.ds(row + PAD, 1), :]
        return carry

    lax.fori_loop(0, count // UNROLL, some, 0)


def parcel_of(rows):
    return rows.T[:ROWS]


def rows_of(parcel):
    halo = parcel.shape[1]
    return jnp.concatenate([parcel, jnp.zeros((LANES - ROWS, halo), F32)], axis=0).T


def scaled_volume(vol, flag, stretch, scaled):
    nv = vol.shape[1]
    tilt = flag[...].astype(F32) * stretch[...]
    real, imag = vol[0], vol[1]
    fill = jnp.zeros((LANES - nv, vol.shape[2]), F32)
    scaled[0:nv, :] = real - tilt * imag
    scaled[nv:LANES, :] = fill
    scaled[LANES : LANES + nv, :] = imag + tilt * real
    scaled[LANES + nv : 2 * LANES, :] = fill


def prepare_kernel(
    vol, flag, stretch, trace, cond_op, elem_face, halo_list,
    table, own_sum, up, mid, down,
    scaled, turned, matrix, matrix_hi, matrix_lo, parts, sums0, sums1, sums2, sums3, picked,
):
    nq, faces = trace.shape[1], trace.shape[2]
    nv, elems = vol.shape[1], vol.shape[2]
    halo = halo_list.shape[1]
    turned[...] = jnp.zeros_like(turned)
    turned[0:nq, :] = trace[0]
    turned[HALF : HALF + nq, :] = trace[1]
    table[0:PAD, :] = jnp.zeros((PAD, LANES), F32)
    for first in range(0, faces, LANES):
        table[PAD + first : PAD + first + LANES, :] = turned[:, first : first + LANES].T
    scaled_volume(vol, flag, stretch, scaled)
    matrix[...] = jnp.zeros_like(matrix)
    for corner in range(4):
        low = corner * LANES
        matrix[low : low + nq, 0:nv] = cond_op[corner, 0]
        matrix[low : low + nq, LANES : LANES + nv] = -cond_op[corner, 1]
        matrix[low + HALF : low + HALF + nq, 0:nv] = cond_op[corner, 1]
        matrix[low + HALF : low + HALF + nq, LANES : LANES + nv] = cond_op[corner, 0]
    high, rest = split(matrix[...])
    matrix_hi[...] = high
    matrix_lo[...] = rest
    for first in range(0, elems, LANES):
        stop = first + LANES
        columns = jnp.concatenate(
            [scaled[0:LANES, first:stop].T, scaled[LANES : 2 * LANES, first:stop].T], axis=1
        )
        high, rest = split(columns)
        product = (
            dot(high, matrix_hi[...], 1, 1)
            + dot(rest, matrix_hi[...], 1, 1)
            + dot(high, matrix_lo[...], 1, 1)
        )
        for corner in range(4):
            parts[corner, first:stop, :] = product[:, corner * LANES : (corner + 1) * LANES]
    sums = (sums0, sums1, sums2, sums3)
    for total in sums:
        total[...] = jnp.zeros_like(total)

    def add_some(step, carry):
        for extra in range(4):
            elem = step * 4 + extra
            for corner in range(4):
                slot = elem_face[corner, elem]
                total = sums[corner]
                total[pl.ds(slot, 1), :] = (
                    total[pl.ds(slot, 1), :] + parts[corner, pl.ds(elem, 1), :]
                )
        return carry

    lax.fori_loop(0, elems // 4, add_some, 0)

    def summed(first, size):
        stop = first + size
        return (sums0[first:stop] + sums1[first:stop]) + (sums2[first:stop] + sums3[first:stop])

    own_sum[...] = summed(0, faces)
    for direction in range(DIRS):
        gather_rows(
            halo, lambda j: halo_list[direction, j], table, picked, direction * halo
        )
    for direction in range(DIRS):
        parcel = parcel_of(picked[direction * halo : (direction + 1) * halo, :])
        back = parcel_of(summed(faces + direction * halo, halo))
        if direction < 3:
            down[direction] = parcel
            up[3 + direction] = back
        elif direction < 5:
            mid[direction - 3] = parcel
            mid[direction - 1] = back
        else:
            up[direction - 5] = parcel
            down[direction - 2] = back


def skeleton_matrix(skel_op, matrix):
    nq = skel_op.shape[2]
    for block in range(skel_op.shape[0]):
        real, real_moved = half_rolled(skel_op[block, 0], nq)
        imag, imag_moved = half_rolled(skel_op[block, 1], nq)
        fill = jnp.zeros((HALF - nq, LANES), F32)
        whole = jnp.concatenate([real - imag_moved, fill, imag + real_moved, fill], axis=0)
        high, rest = split(whole)
        low = block * 2 * ROWS
        matrix[low : low + 2 * ROWS, :] = jnp.concatenate(
            [
                jnp.concatenate([high, high], axis=1),
                jnp.concatenate([rest, jnp.zeros_like(rest)], axis=1),
            ],
            axis=0,
        )


def skeleton_tile(matrix, block_coef, source_of, first, size):
    real_sum = jnp.zeros((HALF, size), F32)
    imag_sum = jnp.zeros((HALF, size), F32)
    for block in range(block_coef.shape[0]):
        high, rest = split(source_of(block, first, size))
        low = block * 2 * ROWS
        product = dot(
            matrix[low : low + 2 * ROWS, :], jnp.concatenate([high, rest], axis=1), 1, 1
        )
        real = product[0:HALF] + product[ROWS : ROWS + HALF]
        imag = product[HALF:ROWS] + product[ROWS + HALF : 2 * ROWS]
        coef_real = block_coef[block, 0:1, pl.ds(first, size)]
        coef_imag = block_coef[block, 1:2, pl.ds(first, size)]
        real_sum = real_sum + (coef_real * real - coef_imag * imag)
        imag_sum = imag_sum + (coef_real * imag + coef_imag * real)
    return real_sum, imag_sum


def gather_neighbours(adjacency, slots, picked):
    count, faces = adjacency.shape
    for neighbour in range(count):
        gather_rows(
            faces, lambda j: adjacency[neighbour, j], slots, picked, neighbour * faces
        )


def residual_kernel(
    table, own_sum, up, down, right, left, skel_op, block_coef, adjacency, halo_list,
    slots, rest_table, res_up, res_mid, res_down,
    picked, matrix, back, sums0, sums1, sums2, sums3,
):
    faces = adjacency.shape[1]
    halo = halo_list.shape[1]
    ghosts = (left[0], down[1], right[0], left[1], right[1], left[2], up[1], right[2])
    slots[0 : PAD + faces, :] = table[...]
    for direction in range(DIRS):
        first = PAD + faces + direction * halo
        slots[first : first + halo, :] = rows_of(ghosts[direction])
    returned = (right[3], up[4], left[3], right[4], left[4], right[5], down[4], left[5])
    for direction in range(DIRS):
        back[direction] = rows_of(returned[direction])
    skeleton_matrix(skel_op, matrix)
    gather_neighbours(adjacency, slots, picked)
    tile = 256

    def source_of(block, first, size):
        if block == 0:
            return slots[pl.ds(PAD + first, size), :]
        return picked[pl.ds((block - 1) * faces + first, size), :]

    def some(step, carry):
        first = pl.multiple_of(step * tile, tile)
        real, imag = skeleton_tile(matrix, block_coef, source_of, first, tile)
        applied = rows_of(jnp.concatenate([real, imag], axis=0))
        sums0[pl.ds(PAD + first, tile), :] = own_sum[pl.ds(first, tile), :] - applied
        return carry

    lax.fori_loop(0, faces // tile, some, 0)
    sums0[0:PAD, :] = jnp.zeros((PAD, LANES), F32)
    others = (sums1, sums2, sums3)
    for total in others:
        total[...] = jnp.zeros_like(total)
    sums = (sums0,) + others

    def add_some(step, carry):
        for extra in range(2):
            entry = step * 2 + extra
            for direction in range(DIRS):
                face = halo_list[direction, entry] + PAD
                total = sums[direction % 4]
                total[pl.ds(face, 1), :] = (
                    total[pl.ds(face, 1), :] + back[direction, pl.ds(entry, 1), :]
                )
        return carry

    lax.fori_loop(0, halo // 2, add_some, 0)
    rest_table[...] = (sums0[...] + sums1[...]) + (sums2[...] + sums3[...])
    rest_table[0:PAD, :] = jnp.zeros((PAD, LANES), F32)
    for direction in range(DIRS):
        gather_rows(
            halo, lambda j: halo_list[direction, j], rest_table, picked, direction * halo
        )
    for direction in range(DIRS):
        parcel = parcel_of(picked[direction * halo : (direction + 1) * halo, :])
        if direction < 3:
            res_down[direction] = parcel
        elif direction < 5:
            res_mid[direction - 3] = parcel
        else:
            res_up[direction - 5] = parcel


def turn_kernel(rest_table, turned):
    for first in range(0, turned.shape[1], LANES):
        turned[:, first : first + LANES] = parcel_of(
            rest_table[PAD + first : PAD + first + LANES, :]
        )


def recon_kernel(vol, flag, stretch, recon_op, base, scaled, matrix):
    nv, elems = vol.shape[1], vol.shape[2]
    scaled_volume(vol, flag, stretch, scaled)
    matrix[...] = jnp.zeros_like(matrix)
    matrix[0:nv, 0:nv] = recon_op[0]
    matrix[0:nv, LANES : LANES + nv] = -recon_op[1]
    matrix[LANES : LANES + nv, 0:nv] = recon_op[1]
    matrix[LANES : LANES + nv, LANES : LANES + nv] = recon_op[0]
    high, rest = split(matrix[...])
    for first in range(0, elems, 256):
        wanted, fine = split(scaled[:, first : first + 256])
        product = dot(high, wanted) + dot(high, fine) + dot(rest, wanted)
        base[0, :, first : first + 256] = product[0:nv]
        base[1, :, first : first + 256] = product[LANES : LANES + nv]


def image_kernel(
    rest_table, turned, up, down, right, left, skel_op, block_coef, adjacency,
    slots, partial,
    picked, matrix,
):
    faces = adjacency.shape[1]
    halo = up.shape[2]
    ghosts = (left[0], down[1], right[0], left[1], right[1], left[2], up[1], right[2])
    slots[0 : PAD + faces, :] = rest_table[...]
    for direction in range(DIRS):
        first = PAD + faces + direction * halo
        slots[first : first + halo, :] = rows_of(ghosts[direction])
    skeleton_matrix(skel_op, matrix)
    gather_neighbours(adjacency, slots, picked)
    tile = 256

    def source_of(block, first, size):
        if block == 0:
            return slots[pl.ds(PAD + first, size), :]
        return picked[pl.ds((block - 1) * faces + first, size), :]

    def some(step, carry):
        first = pl.multiple_of(step * tile, tile)
        real, imag = skeleton_tile(matrix, block_coef, source_of, first, tile)
        rest_real = turned[0:HALF, pl.ds(first, tile)]
        rest_imag = turned[HALF:ROWS, pl.ds(first, tile)]
        return (
            carry[0] + (real * rest_real + imag * rest_imag),
            carry[1] + (real * rest_imag - imag * rest_real),
            carry[2] + (real * real + imag * imag),
        )

    zero = jnp.zeros((HALF, tile), F32)
    totals = lax.fori_loop(0, faces // tile, some, (zero, zero, zero))
    lane = lax.broadcasted_iota(jnp.int32, (1, LANES), 1)
    line = jnp.zeros((1, LANES), F32)
    for place in range(3):
        line = line + jnp.where(lane == place, jnp.sum(totals[place]), 0.0)
    partial[...] = line


def finish_kernel(
    gathered, trace, turned, slots_trace, slots_rest, lift_op, base, elem_face,
    trace_out, volume_out,
    slots, picked, matrix,
):
    nq = trace.shape[1]
    nv, elems = base.shape[1], base.shape[2]
    line = jnp.sum(gathered[...], axis=0, keepdims=True)
    lane = lax.broadcasted_iota(jnp.int32, (1, LANES), 1)
    entry = [
        jnp.sum(jnp.where(lane == place, line, 0.0), axis=1, keepdims=True)
        for place in range(3)
    ]
    step_real = entry[0] / entry[2]
    step_imag = entry[1] / entry[2]
    rest_real = turned[0:nq, :]
    rest_imag = turned[HALF : HALF + nq, :]
    trace_out[0] = trace[0] + (step_real * rest_real - step_imag * rest_imag)
    trace_out[1] = trace[1] + (step_real * rest_imag + step_imag * rest_real)
    for block in range(4):
        real, real_moved = half_rolled(lift_op[block, 0], nv)
        imag, imag_moved = half_rolled(lift_op[block, 1], nv)
        fill = jnp.zeros((LANES - nv, LANES), F32)
        high, rest = split(
            jnp.concatenate([real - imag_moved, fill, imag + real_moved, fill], axis=0)
        )
        low = block * 4 * LANES
        matrix[low : low + 4 * LANES, :] = jnp.concatenate(
            [
                jnp.concatenate([high, high], axis=1),
                jnp.concatenate([rest, jnp.zeros_like(rest)], axis=1),
            ],
            axis=0,
        )
    size = 256
    is_real = lax.broadcasted_iota(jnp.int32, (size, LANES), 1) < HALF

    def new_rows(step, carry):
        first = pl.multiple_of(PAD + step * size, PAD)
        rest_rows = slots_rest[pl.ds(first, size), :]
        turn = jnp.where(
            is_real, -pltpu.roll(rest_rows, LANES - HALF, 1), pltpu.roll(rest_rows, HALF, 1)
        )
        slots[pl.ds(first, size), :] = slots_trace[pl.ds(first, size), :] + (
            step_real * rest_rows + step_imag * turn
        )
        return carry

    lax.fori_loop(0, (slots.shape[0] - PAD) // size, new_rows, 0)
    for corner in range(4):
        gather_rows(elems, lambda j: elem_face[corner, j], slots, picked, corner * elems)
    for first in range(0, elems, size):
        total = jnp.zeros((2 * LANES, size), F32)
        for corner in range(4):
            low = corner * elems + first
            rows = jnp.concatenate(
                [picked[low : low + size, 0:LANES]], axis=1
            )
            high, rest = split(rows)
            at = corner * 4 * LANES
            product = dot(
                matrix[at : at + 4 * LANES, :], jnp.concatenate([high, rest], axis=1), 1, 1
            )
            total = total + (product[0 : 2 * LANES] + product[2 * LANES : 4 * LANES])
        stop = first + size
        volume_out[0, :, first:stop] = base[0, :, first:stop] - total[0:nv]
        volume_out[1, :, first:stop] = base[1, :, first:stop] - total[LANES : LANES + nv]


def call(kernel, name, args, out_shapes, scratch, scalars=(), cost=1000000):
    vmem = pl.BlockSpec(memory_space=pltpu.VMEM)
    smem = pl.BlockSpec(memory_space=pltpu.SMEM)
    return pl.pallas_call(
        kernel,
        name=name,
        out_shape=[jax.ShapeDtypeStruct(shape, F32) for shape in out_shapes],
        in_specs=[smem if number in scalars else vmem for number in range(len(args))],
        out_specs=[vmem] * len(out_shapes),
        scratch_shapes=[pltpu.VMEM(shape, kind) for shape, kind in scratch],
        compiler_params=pltpu.CompilerParams(vmem_limit_bytes=56 * MIB),
        cost_estimate=pl.CostEstimate(flops=cost, bytes_accessed=4 * MIB, transcendentals=0),
    )(*args)


def from_behind(block, axis, distance):
    devices = range(lax.axis_size(axis))
    route = [(i - distance, i) for i in devices if i - distance in devices]
    return lax.ppermute(block, axis, route)


def summed_over(line, axis, sizes):
    count = lax.axis_size(axis)
    stride = 1
    for size in sizes:
        if stride == count:
            break
        size = min(size, count // stride)
        groups = [
            [block * size * stride + low + stride * k for k in range(size)]
            for block in range(count // (size * stride))
            for low in range(stride)
        ]
        line = lax.all_gather(jnp.sum(line, axis=0), axis, axis_index_groups=groups)
        stride *= size
    return line


def local(
    vol_rhs, trace_in, pml_flag, stretch, cond_op, skel_op, block_coef, recon_op, lift_op,
    elem_face, adjacency, halo_list,
):
    nv, elems = vol_rhs.shape[1], vol_rhs.shape[2]
    faces = trace_in.shape[2]
    halo = halo_list.shape[1]
    blocks = skel_op.shape[0]
    neighbours = adjacency.shape[0]
    slots = faces + DIRS * halo
    flag = pml_flag.reshape(1, elems)
    tilt = stretch.reshape(1, elems)
    table, own_sum, up, mid, down = call(
        prepare_kernel,
        "prepare",
        (vol_rhs, flag, tilt, trace_in, cond_op, elem_face, halo_list),
        [(PAD + faces, LANES), (faces, LANES), (6, ROWS, halo), (4, ROWS, halo), (6, ROWS, halo)],
        [
            ((2 * LANES, elems), F32),
            ((LANES, faces), F32),
            ((4 * LANES, 2 * LANES), F32),
            ((4 * LANES, 2 * LANES), BF16),
            ((4 * LANES, 2 * LANES), BF16),
            ((4, elems, LANES), F32),
        ]
        + [((slots, LANES), F32)] * 4
        + [((DIRS * halo, LANES), F32)],
        (5, 6),
    )
    up = from_behind(up, "gx", 1)
    down = from_behind(down, "gx", -1)
    (base,) = call(
        recon_kernel,
        "recon",
        (vol_rhs, flag, tilt, recon_op),
        [(2, nv, elems)],
        [((2 * LANES, elems), F32), ((2 * LANES, 2 * LANES), F32)],
    )
    right = jnp.stack([down[2], mid[1], up[2], up[3], mid[2], down[3]])
    left = jnp.stack([down[0], mid[0], up[0], up[5], mid[3], down[5]])
    right = from_behind(right, "gy", 1)
    left = from_behind(left, "gy", -1)
    slots_trace, rest_table, res_up, res_mid, res_down = call(
        residual_kernel,
        "residual",
        (table, own_sum, up, down, right, left, skel_op, block_coef, adjacency, halo_list),
        [(PAD + slots, LANES), (PAD + faces, LANES)]
        + [(3, ROWS, halo), (2, ROWS, halo), (3, ROWS, halo)],
        [
            ((neighbours * faces, LANES), F32),
            ((blocks * 2 * ROWS, 2 * LANES), BF16),
            ((DIRS, halo, LANES), F32),
        ]
        + [((PAD + faces, LANES), F32)] * 4,
        (8, 9),
    )
    res_up = from_behind(res_up, "gx", 1)
    res_down = from_behind(res_down, "gx", -1)
    (turned,) = call(turn_kernel, "turn", (rest_table,), [(ROWS, faces)], [])
    res_right = jnp.stack([res_down[2], res_mid[1], res_up[2]])
    res_left = jnp.stack([res_down[0], res_mid[0], res_up[0]])
    res_right = from_behind(res_right, "gy", 1)
    res_left = from_behind(res_left, "gy", -1)
    slots_rest, partial = call(
        image_kernel,
        "image",
        (
            rest_table, turned, res_up, res_down, res_right, res_left, skel_op, block_coef,
            adjacency,
        ),
        [(PAD + slots, LANES), (1, LANES)],
        [
            ((neighbours * faces, LANES), F32),
            ((blocks * 2 * ROWS, 2 * LANES), BF16),
        ],
        (8,),
    )
    gathered = summed_over(partial, "gy", (2, 4, 4))
    gathered = summed_over(gathered, "gx", (4, 4))
    trace_out, volume_out = call(
        finish_kernel,
        "finish",
        (gathered, trace_in, turned, slots_trace, slots_rest, lift_op, base, elem_face),
        [trace_in.shape, vol_rhs.shape],
        [
            ((PAD + slots, LANES), F32),
            ((4 * elems, LANES), F32),
            ((4 * 4 * LANES, 2 * LANES), BF16),
        ],
        (7,),
    )
    return trace_out, volume_out


def solution(mesh):
    split_last = ("gx", "gy")
    in_specs = (
        P(None, None, split_last),
        P(None, None, split_last),
        P(split_last),
        P(split_last),
        P(),
        P(),
        P(None, None, split_last),
        P(),
        P(),
        P(None, split_last),
        P(None, split_last),
        P(None, split_last),
    )
    out_specs = (P(None, None, split_last), P(None, None, split_last))
    return jax.shard_map(
        local, mesh=mesh, in_specs=in_specs, out_specs=out_specs, check_vma=False
    )
```

```python
import functools

import jax
import jax.numpy as jnp
from jax import lax
from jax.experimental import pallas as pl
from jax.experimental.pallas import tpu as pltpu
from jax.sharding import PartitionSpec as P

F32 = jnp.float32
BF16 = jnp.bfloat16
HALF = 40
ROWS = 2 * HALF
LANES = 128
PAD = 8
DIRS = 8
UNROLL = 128
MIB = 1 << 20


def split(values):
    high = values.astype(BF16)
    return high, (values - high.astype(F32)).astype(BF16)


def dot(left, right, left_dim=1, right_dim=0):
    return lax.dot_general(
        left, right, (((left_dim,), (right_dim,)), ((), ())), preferred_element_type=F32
    )


def half_rolled(block, height):
    wide = jnp.concatenate(
        [block, jnp.zeros((height, LANES - block.shape[1]), F32)], axis=1
    )
    return wide, pltpu.roll(wide, HALF, 1)


def gather_rows(count, indices, source, target):
    def some(step, carry):
        first = step * UNROLL
        for extra in range(UNROLL):
            row = indices[first + extra]
            target[pl.ds(first + extra, 1), :] = source[pl.ds(row + PAD, 1), :]
        return carry

    lax.fori_loop(0, count // UNROLL, some, 0)


def begin(source, target, semaphore):
    copy = pltpu.make_async_copy(source, target, semaphore)
    copy.start()
    return copy


def parcel_of(rows):
    return rows.T[:ROWS]


def rows_of(parcel):
    halo = parcel.shape[1]
    return jnp.concatenate([parcel, jnp.zeros((LANES - ROWS, halo), F32)], axis=0).T


def scaled_volume(vol, flag, stretch, scaled):
    nv = vol.shape[1]
    tilt = flag[...].astype(F32) * stretch[...]
    real, imag = vol[0], vol[1]
    fill = jnp.zeros((LANES - nv, vol.shape[2]), F32)
    scaled[0:nv, :] = real - tilt * imag
    scaled[nv:LANES, :] = fill
    scaled[LANES : LANES + nv, :] = imag + tilt * real
    scaled[LANES + nv : 2 * LANES, :] = fill


def place_parcels(picked, halo, lower, middle, upper):
    for direction in range(DIRS):
        parcel = parcel_of(picked[direction * halo : (direction + 1) * halo, :])
        if direction < 3:
            lower[direction] = parcel
        elif direction < 5:
            middle[direction - 3] = parcel
        else:
            upper[direction - 5] = parcel


def traces_kernel(
    trace, halo_list, table, up, mid, down, rows, turned, picked, done
):
    nq, faces = trace.shape[1], trace.shape[2]
    halo = up.shape[2]
    turned[...] = jnp.zeros_like(turned)
    turned[0:nq, :] = trace[0]
    turned[HALF : HALF + nq, :] = trace[1]
    rows[0:PAD, :] = jnp.zeros((PAD, LANES), F32)
    for first in range(0, faces, LANES):
        rows[PAD + first : PAD + first + LANES, :] = turned[:, first : first + LANES].T
    table_copy = begin(rows, table, done.at[0])
    gather_rows(DIRS * halo, halo_list, rows, picked)
    place_parcels(picked, halo, down, mid, up)
    table_copy.wait()


def sources_kernel(
    vol, flag, stretch, cond_op, elem_face,
    own_sum, up, mid, down,
    own, scaled, matrix, matrix_hi, matrix_lo, parts, sums0, sums1, sums2, sums3, ghosts, done,
):
    faces = own.shape[0]
    halo = up.shape[2]
    nq = cond_op.shape[2]
    nv, elems = vol.shape[1], vol.shape[2]
    scaled_volume(vol, flag, stretch, scaled)
    matrix[...] = jnp.zeros_like(matrix)
    for corner in range(4):
        low = corner * LANES
        matrix[low : low + nq, 0:nv] = cond_op[corner, 0]
        matrix[low : low + nq, LANES : LANES + nv] = -cond_op[corner, 1]
        matrix[low + HALF : low + HALF + nq, 0:nv] = cond_op[corner, 1]
        matrix[low + HALF : low + HALF + nq, LANES : LANES + nv] = cond_op[corner, 0]
    high, rest = split(matrix[...])
    matrix_hi[...] = high
    matrix_lo[...] = rest
    for first in range(0, elems, LANES):
        stop = first + LANES
        columns = jnp.concatenate(
            [scaled[0:LANES, first:stop].T, scaled[LANES : 2 * LANES, first:stop].T], axis=1
        )
        high, rest = split(columns)
        product = (
            dot(high, matrix_hi[...], 1, 1)
            + dot(rest, matrix_hi[...], 1, 1)
            + dot(high, matrix_lo[...], 1, 1)
        )
        for corner in range(4):
            parts[corner, first:stop, :] = product[:, corner * LANES : (corner + 1) * LANES]
    sums = (sums0, sums1, sums2, sums3)
    for total in sums:
        total[...] = jnp.zeros_like(total)

    def add_some(step, carry):
        for extra in range(4):
            elem = step * 4 + extra
            for corner in range(4):
                slot = elem_face[corner * elems + elem]
                total = sums[corner]
                total[pl.ds(slot, 1), :] = (
                    total[pl.ds(slot, 1), :] + parts[corner, pl.ds(elem, 1), :]
                )
        return carry

    lax.fori_loop(0, elems // 4, add_some, 0)

    def summed(first, size):
        stop = first + size
        return (sums0[first:stop] + sums1[first:stop]) + (sums2[first:stop] + sums3[first:stop])

    own[...] = summed(0, faces)
    own_copy = begin(own, own_sum, done.at[0])
    ghosts[...] = summed(faces, DIRS * halo)
    place_parcels(ghosts, halo, up, mid, down)
    own_copy.wait()


def skeleton_matrix(skel_op, matrix):
    nq = skel_op.shape[2]
    for block in range(skel_op.shape[0]):
        real, real_moved = half_rolled(skel_op[block, 0], nq)
        imag, imag_moved = half_rolled(skel_op[block, 1], nq)
        fill = jnp.zeros((HALF - nq, LANES), F32)
        whole = jnp.concatenate([real - imag_moved, fill, imag + real_moved, fill], axis=0)
        high, rest = split(whole)
        low = block * 2 * ROWS
        matrix[low : low + 2 * ROWS, :] = jnp.concatenate(
            [
                jnp.concatenate([high, high], axis=1),
                jnp.concatenate([rest, jnp.zeros_like(rest)], axis=1),
            ],
            axis=0,
        )


def skeleton_tile(matrix, block_coef, source_of, first, size):
    real_sum = jnp.zeros((HALF, size), F32)
    imag_sum = jnp.zeros((HALF, size), F32)
    for block in range(block_coef.shape[0]):
        high, rest = split(source_of(block, first, size))
        low = block * 2 * ROWS
        product = dot(
            matrix[low : low + 2 * ROWS, :], jnp.concatenate([high, rest], axis=1), 1, 1
        )
        real = product[0:HALF] + product[ROWS : ROWS + HALF]
        imag = product[HALF:ROWS] + product[ROWS + HALF : 2 * ROWS]
        coef_real = block_coef[block, 0:1, pl.ds(first, size)]
        coef_imag = block_coef[block, 1:2, pl.ds(first, size)]
        real_sum = real_sum + (coef_real * real - coef_imag * imag)
        imag_sum = imag_sum + (coef_real * imag + coef_imag * real)
    return real_sum, imag_sum


def join_kernel(up, mid, down, right, left, done):
    moves = [(down, 2, right, 0), (mid, 1, right, 1), (up, 2, right, 2)]
    moves += [(down, 0, left, 0), (mid, 0, left, 1), (up, 0, left, 2)]
    copies = [
        begin(source.at[place], target.at[to], done.at[number])
        for number, (source, place, target, to) in enumerate(moves)
    ]
    for copy in copies:
        copy.wait()


def ghost_places(up, down, right, left):
    return (
        left.at[0], down.at[1], right.at[0], left.at[1],
        right.at[1], left.at[2], up.at[1], right.at[2],
    )


def apply_kernel(
    table, own_sum, up, down, right, left, skel_op, block_coef, adjacency,
    slots_out, rest_out,
    slots, own, rest, arrived, picked, matrix, done,
):
    faces = own.shape[0]
    halo = arrived.shape[2]
    table_copy = begin(table, slots.at[pl.ds(0, PAD + faces)], done.at[0])
    copies = [
        begin(place, arrived.at[direction], done.at[3 + direction])
        for direction, place in enumerate(ghost_places(up, down, right, left))
    ]
    own_copy = begin(own_sum, own, done.at[1])
    skeleton_matrix(skel_op, matrix)
    for direction in range(DIRS):
        copies[direction].wait()
        first = PAD + faces + direction * halo
        slots[first : first + halo, :] = rows_of(arrived[direction])
    table_copy.wait()
    slots_copy = begin(slots, slots_out, done.at[2])
    gather_rows(adjacency.shape[0], adjacency, slots, picked)
    own_copy.wait()
    tile = 256

    def source_of(block, first, size):
        if block == 0:
            return slots[pl.ds(PAD + first, size), :]
        return picked[pl.ds((block - 1) * faces + first, size), :]

    def some(step, carry):
        first = pl.multiple_of(step * tile, tile)
        real, imag = skeleton_tile(matrix, block_coef, source_of, first, tile)
        applied = rows_of(jnp.concatenate([real, imag], axis=0))
        rest[pl.ds(first, tile), :] = own[pl.ds(first, tile), :] - applied
        return carry

    lax.fori_loop(0, faces // tile, some, 0)
    begin(rest, rest_out, done.at[0]).wait()
    slots_copy.wait()


def residual_kernel(
    rest, up, down, right, left, halo_list,
    rest_table, res_up, res_mid, res_down,
    returned, picked, back, sums0, sums1, sums2, sums3, done,
):
    faces = rest.shape[0]
    halo = returned.shape[2]
    rest_copy = begin(rest, sums0.at[pl.ds(PAD, faces)], done.at[0])
    places = (
        left.at[2], up.at[1], right.at[2], left.at[1],
        right.at[1], left.at[0], down.at[1], right.at[0],
    )
    copies = [
        begin(place, returned.at[direction], done.at[1 + direction])
        for direction, place in enumerate(places)
    ]
    sums0[0:PAD, :] = jnp.zeros((PAD, LANES), F32)
    others = (sums1, sums2, sums3)
    for total in others:
        total[...] = jnp.zeros_like(total)
    for direction in range(DIRS):
        copies[direction].wait()
        back[direction] = rows_of(returned[direction])
    rest_copy.wait()
    sums = (sums0,) + others

    def add_some(step, carry):
        for extra in range(2):
            entry = step * 2 + extra
            for direction in range(DIRS):
                face = halo_list[direction * halo + entry] + PAD
                total = sums[direction % 4]
                total[pl.ds(face, 1), :] = (
                    total[pl.ds(face, 1), :] + back[direction, pl.ds(entry, 1), :]
                )
        return carry

    lax.fori_loop(0, halo // 2, add_some, 0)
    rest_table[...] = (sums0[...] + sums1[...]) + (sums2[...] + sums3[...])
    rest_table[0:PAD, :] = jnp.zeros((PAD, LANES), F32)
    gather_rows(DIRS * halo, halo_list, rest_table, picked)
    place_parcels(picked, halo, res_down, res_mid, res_up)


def turn_kernel(rest_table, turned):
    for first in range(0, turned.shape[1], LANES):
        turned[:, first : first + LANES] = parcel_of(
            rest_table[PAD + first : PAD + first + LANES, :]
        )


def lift_matrix(lift_op, matrix):
    nv = lift_op.shape[2]
    for corner in range(4):
        real, real_moved = half_rolled(lift_op[corner, 0], nv)
        imag, imag_moved = half_rolled(lift_op[corner, 1], nv)
        fill = jnp.zeros((LANES - nv, LANES), F32)
        high, rest = split(
            jnp.concatenate([real - imag_moved, fill, imag + real_moved, fill], axis=0)
        )
        low = corner * 4 * LANES
        matrix[low : low + 4 * LANES, :] = jnp.concatenate(
            [
                jnp.concatenate([high, high], axis=1),
                jnp.concatenate([rest, jnp.zeros_like(rest)], axis=1),
            ],
            axis=0,
        )


def lifted_tile(matrix, picked, elems, first, size):
    total = jnp.zeros((2 * LANES, size), F32)
    for corner in range(4):
        low = corner * elems + first
        high, rest = split(picked[low : low + size, :])
        at = corner * 4 * LANES
        product = dot(
            matrix[at : at + 4 * LANES, :], jnp.concatenate([high, rest], axis=1), 1, 1
        )
        total = total + (product[0 : 2 * LANES] + product[2 * LANES : 4 * LANES])
    return total


def base_kernel(
    slots_in, vol, flag, stretch, recon_op, lift_op, elem_face,
    base,
    slots, picked, scaled, recon, matrix, done,
):
    nv, elems = vol.shape[1], vol.shape[2]
    slots_copy = begin(slots_in, slots, done.at[0])
    lift_matrix(lift_op, matrix)
    scaled_volume(vol, flag, stretch, scaled)
    recon[...] = jnp.zeros_like(recon)
    recon[0:nv, 0:nv] = recon_op[0]
    recon[0:nv, LANES : LANES + nv] = -recon_op[1]
    recon[LANES : LANES + nv, 0:nv] = recon_op[1]
    recon[LANES : LANES + nv, LANES : LANES + nv] = recon_op[0]
    recon_high, recon_rest = split(recon[...])
    slots_copy.wait()
    gather_rows(4 * elems, elem_face, slots, picked)
    size = 256
    for first in range(0, elems, size):
        stop = first + size
        wanted, fine = split(scaled[:, first:stop])
        product = dot(recon_high, wanted) + dot(recon_high, fine) + dot(recon_rest, wanted)
        product = product - lifted_tile(matrix, picked, elems, first, size)
        base[0, :, first:stop] = product[0:nv]
        base[1, :, first:stop] = product[LANES : LANES + nv]


def lift_kernel(slots_in, lift_op, elem_face, lifted, slots, picked, matrix, done):
    nv, elems = lifted.shape[1], lifted.shape[2]
    slots_copy = begin(slots_in, slots, done.at[0])
    lift_matrix(lift_op, matrix)
    slots_copy.wait()
    gather_rows(4 * elems, elem_face, slots, picked)
    size = 256
    for first in range(0, elems, size):
        stop = first + size
        product = lifted_tile(matrix, picked, elems, first, size)
        lifted[0, :, first:stop] = product[0:nv]
        lifted[1, :, first:stop] = product[LANES : LANES + nv]


def image_kernel(
    rest_table, turned, up, down, right, left, skel_op, block_coef, adjacency,
    slots_out, partial,
    slots, arrived, picked, matrix, done,
):
    faces = turned.shape[1]
    halo = arrived.shape[2]
    table_copy = begin(rest_table, slots.at[pl.ds(0, PAD + faces)], done.at[0])
    copies = [
        begin(place, arrived.at[direction], done.at[3 + direction])
        for direction, place in enumerate(ghost_places(up, down, right, left))
    ]
    skeleton_matrix(skel_op, matrix)
    for direction in range(DIRS):
        copies[direction].wait()
        first = PAD + faces + direction * halo
        slots[first : first + halo, :] = rows_of(arrived[direction])
    table_copy.wait()
    slots_copy = begin(slots, slots_out, done.at[2])
    gather_rows(adjacency.shape[0], adjacency, slots, picked)
    tile = 256

    def source_of(block, first, size):
        if block == 0:
            return slots[pl.ds(PAD + first, size), :]
        return picked[pl.ds((block - 1) * faces + first, size), :]

    def some(step, carry):
        first = pl.multiple_of(step * tile, tile)
        real, imag = skeleton_tile(matrix, block_coef, source_of, first, tile)
        rest_real = turned[0:HALF, pl.ds(first, tile)]
        rest_imag = turned[HALF:ROWS, pl.ds(first, tile)]
        return (
            carry[0] + (real * rest_real + imag * rest_imag),
            carry[1] + (real * rest_imag - imag * rest_real),
            carry[2] + (real * real + imag * imag),
        )

    zero = jnp.zeros((HALF, tile), F32)
    totals = lax.fori_loop(0, faces // tile, some, (zero, zero, zero))
    lane = lax.broadcasted_iota(jnp.int32, (1, LANES), 1)
    line = jnp.zeros((1, LANES), F32)
    for place in range(3):
        line = line + jnp.where(lane == place, jnp.sum(totals[place]), 0.0)
    partial[...] = jnp.broadcast_to(line, partial.shape)
    slots_copy.wait()


def finish_kernel(gathered, trace, turned, base, lifted, trace_out, volume_out):
    nq = trace.shape[1]
    line = jnp.sum(gathered[...], axis=0, keepdims=True)
    lane = lax.broadcasted_iota(jnp.int32, (1, LANES), 1)
    entry = [
        jnp.sum(jnp.where(lane == place, line, 0.0), axis=1, keepdims=True)
        for place in range(3)
    ]
    step_real = entry[0] / entry[2]
    step_imag = entry[1] / entry[2]
    volume_out[0] = base[0] - (step_real * lifted[0] - step_imag * lifted[1])
    volume_out[1] = base[1] - (step_real * lifted[1] + step_imag * lifted[0])
    rest_real = turned[0:nq, :]
    rest_imag = turned[HALF : HALF + nq, :]
    trace_out[0] = trace[0] + (step_real * rest_real - step_imag * rest_imag)
    trace_out[1] = trace[1] + (step_real * rest_imag + step_imag * rest_real)


SPACES = {
    "v": pltpu.MemorySpace.VMEM,
    "s": pltpu.MemorySpace.SMEM,
    "a": pl.ANY,
    "h": pltpu.HBM,
    "V": pltpu.MemorySpace.VMEM,
}


def call(kernel, name, args, out_shapes, spaces, scratch, limit, semaphores=0, time=1):
    specs = [pl.BlockSpec(memory_space=SPACES[letter]) for letter in spaces]
    shapes = [pltpu.VMEM(shape, kind) for shape, kind in scratch]
    if semaphores:
        shapes.append(pltpu.SemaphoreType.DMA((semaphores,)))
    args = [
        pltpu.with_memory_space_constraint(arg, pltpu.HBM) if letter in "hV" else arg
        for arg, letter in zip(args, spaces)
    ]
    return pl.pallas_call(
        kernel,
        name=name,
        out_shape=[
            pltpu.HBM(shape, F32) if letter in "hV" else jax.ShapeDtypeStruct(shape, F32)
            for shape, letter in zip(out_shapes, spaces[len(args) :])
        ],
        in_specs=specs[: len(args)],
        out_specs=specs[len(args) :],
        scratch_shapes=shapes,
        compiler_params=pltpu.CompilerParams(vmem_limit_bytes=limit * MIB),
        cost_estimate=pl.CostEstimate(
            flops=0, bytes_accessed=3300000 * time, transcendentals=0
        ),
    )(*args)


def from_behind(block, axis, distance):
    devices = range(lax.axis_size(axis))
    route = [(i - distance, i) for i in devices if i - distance in devices]
    return lax.ppermute(block, axis, route)


def everywhere(lines, axis):
    return lax.all_to_all(lines, axis, 0, 0)


def local(
    vol_rhs, trace_in, pml_flag, stretch, cond_op, skel_op, block_coef, recon_op, lift_op,
    elem_face, adjacency, halo_list,
):
    nv, elems = vol_rhs.shape[1], vol_rhs.shape[2]
    faces = trace_in.shape[2]
    halo = halo_list.shape[1]
    blocks = skel_op.shape[0]
    neighbours = adjacency.shape[0]
    slots = faces + DIRS * halo
    elem_face = elem_face.reshape(-1)
    adjacency = adjacency.reshape(-1)
    halo_list = halo_list.reshape(-1)
    flag = pml_flag.reshape(1, elems)
    tilt = stretch.reshape(1, elems)
    parcels = [(3, ROWS, halo), (2, ROWS, halo), (3, ROWS, halo)]

    def exchange(up, mid, down, sign, beside=None):
        up = from_behind(up, "gx", 1)
        down = from_behind(down, "gx", -1)
        if beside is not None:
            up, down, beside = lax.optimization_barrier((up, down, beside))
        right, left = call(
            join_kernel, "join", (up, mid, down), [up.shape, up.shape], "aaa" + "vv", [], 2, 6
        )
        right = from_behind(right, "gy", sign)
        left = from_behind(left, "gy", -sign)
        return (up, down, right, left) if beside is None else (up, down, right, left, beside)

    table, *outgoing = call(
        traces_kernel,
        "traces",
        (trace_in, halo_list),
        [(PAD + faces, LANES)] + parcels,
        "vs" + "hvvv",
        [((PAD + faces, LANES), F32), ((LANES, faces), F32), ((DIRS * halo, LANES), F32)],
        8,
        1,
        4,
    )
    arrived = exchange(*outgoing, 1)
    own_sum, *outgoing = call(
        sources_kernel,
        "sources",
        (vol_rhs, flag, tilt, cond_op, elem_face),
        [(faces, LANES)] + parcels,
        "VVVVs" + "hvvv",
        [
            ((faces, LANES), F32),
            ((2 * LANES, elems), F32),
            ((4 * LANES, 2 * LANES), F32),
            ((4 * LANES, 2 * LANES), BF16),
            ((4 * LANES, 2 * LANES), BF16),
            ((4, elems, LANES), F32),
        ]
        + [((slots, LANES), F32)] * 4
        + [((DIRS * halo, LANES), F32)],
        22,
        1,
        9,
    )
    returned = exchange(*outgoing, -1)
    slots_trace, rest = call(
        apply_kernel,
        "apply",
        (table, own_sum, *arrived, skel_op, block_coef, adjacency),
        [(PAD + slots, LANES), (faces, LANES)],
        "hhaaaaVVs" + "hh",
        [
            ((PAD + slots, LANES), F32),
            ((faces, LANES), F32),
            ((faces, LANES), F32),
            ((DIRS, ROWS, halo), F32),
            ((neighbours * faces, LANES), F32),
            ((blocks * 2 * ROWS, 2 * LANES), BF16),
        ],
        20,
        3 + DIRS,
        18,
    )
    rest_table, *outgoing = call(
        residual_kernel,
        "residual",
        (rest, *returned, halo_list),
        [(PAD + faces, LANES)] + parcels,
        "haaaas" + "Vvvv",
        [
            ((DIRS, ROWS, halo), F32),
            ((DIRS * halo, LANES), F32),
            ((DIRS, halo, LANES), F32),
        ]
        + [((PAD + faces, LANES), F32)] * 4,
        12,
        1 + DIRS,
        8,
    )
    (base,) = call(
        base_kernel,
        "base",
        (slots_trace, vol_rhs, flag, tilt, recon_op, lift_op, elem_face),
        [vol_rhs.shape],
        "hVVVVVs" + "V",
        [
            ((PAD + slots, LANES), F32),
            ((4 * elems, LANES), F32),
            ((2 * LANES, elems), F32),
            ((2 * LANES, 2 * LANES), F32),
            ((4 * 4 * LANES, 2 * LANES), BF16),
        ],
        14,
        1,
        8,
    )
    *arrived, base = exchange(*outgoing, 1, base)
    (turned,) = call(
        turn_kernel, "turn", (rest_table,), [(ROWS, faces)], "VV", [], 4
    )
    across, along = lax.axis_size("gx"), lax.axis_size("gy")
    slots_rest, partial = call(
        image_kernel,
        "image",
        (rest_table, turned, *arrived, skel_op, block_coef, adjacency),
        [(PAD + slots, LANES), (along, LANES)],
        "hVaaaaVVs" + "hv",
        [
            ((PAD + slots, LANES), F32),
            ((DIRS, ROWS, halo), F32),
            ((neighbours * faces, LANES), F32),
            ((blocks * 2 * ROWS, 2 * LANES), BF16),
        ],
        20,
        3 + DIRS,
        18,
    )
    (lifted,) = call(
        lift_kernel,
        "lift",
        (slots_rest, lift_op, elem_face),
        [vol_rhs.shape],
        "hVs" + "V",
        [
            ((PAD + slots, LANES), F32),
            ((4 * elems, LANES), F32),
            ((4 * 4 * LANES, 2 * LANES), BF16),
        ],
        12,
        1,
        7,
    )
    lines, lifted = lax.optimization_barrier((everywhere(partial, "gy"), lifted))
    lines = jnp.sum(lines, axis=0, keepdims=True)
    gathered = everywhere(jnp.broadcast_to(lines, (across, LANES)), "gx")
    trace_out, volume_out = call(
        finish_kernel,
        "finish",
        (gathered, trace_in, turned, base, lifted),
        [trace_in.shape, vol_rhs.shape],
        "vVVVV" + "vV",
        [],
        8,
    )
    return trace_out, volume_out


def solution(mesh):
    split_last = ("gx", "gy")
    in_specs = (
        P(None, None, split_last),
        P(None, None, split_last),
        P(split_last),
        P(split_last),
        P(),
        P(),
        P(None, None, split_last),
        P(),
        P(),
        P(None, split_last),
        P(None, split_last),
        P(None, split_last),
    )
    out_specs = (P(None, None, split_last), P(None, None, split_last))
    return jax.shard_map(
        local, mesh=mesh, in_specs=in_specs, out_specs=out_specs, check_vma=False
    )
```

```python
import functools

import jax
import jax.numpy as jnp
from jax import lax
from jax.experimental import pallas as pl
from jax.experimental.pallas import tpu as pltpu
from jax.sharding import PartitionSpec as P

F32 = jnp.float32
BF16 = jnp.bfloat16
HALF = 40
ROWS = 2 * HALF
LANES = 128
PAD = 8
DIRS = 8
UNROLL = 128
TILE = 256
LIFT = 256
MIB = 1 << 20


def split(values):
    high = values.astype(BF16)
    return high, (values - high.astype(F32)).astype(BF16)


def dot(left, right, left_dim=1, right_dim=0):
    return lax.dot_general(
        left, right, (((left_dim,), (right_dim,)), ((), ())), preferred_element_type=F32
    )


def half_rolled(block, height):
    wide = jnp.concatenate(
        [block, jnp.zeros((height, LANES - block.shape[1]), F32)], axis=1
    )
    return wide, pltpu.roll(wide, HALF, 1)


def gather_rows(count, indices, source, target, start=0, base=0):
    def some(step, carry):
        first = step * UNROLL
        for extra in range(UNROLL):
            row = indices[start + first + extra]
            target[pl.ds(base + first + extra, 1), :] = source[pl.ds(row + PAD, 1), :]
        return carry

    lax.fori_loop(0, count // UNROLL, some, 0)


def begin(source, target, semaphore):
    copy = pltpu.make_async_copy(source, target, semaphore)
    copy.start()
    return copy


def parcel_of(rows):
    return rows.T[:ROWS]


def rows_of(parcel):
    halo = parcel.shape[1]
    return jnp.concatenate([parcel, jnp.zeros((LANES - ROWS, halo), F32)], axis=0).T


def scaled_volume(vol, flag, stretch, scaled):
    nv = vol.shape[1]
    tilt = flag[...].astype(F32) * stretch[...]
    real, imag = vol[0], vol[1]
    fill = jnp.zeros((LANES - nv, vol.shape[2]), F32)
    scaled[0:nv, :] = real - tilt * imag
    scaled[nv:LANES, :] = fill
    scaled[LANES : LANES + nv, :] = imag + tilt * real
    scaled[LANES + nv : 2 * LANES, :] = fill


def place_parcels(picked, halo, lower, middle, upper):
    for direction in range(DIRS):
        parcel = parcel_of(picked[direction * halo : (direction + 1) * halo, :])
        if direction < 3:
            lower[direction] = parcel
        elif direction < 5:
            middle[direction - 3] = parcel
        else:
            upper[direction - 5] = parcel


def traces_kernel(
    trace, halo_list, table, up, mid, down, rows, turned, picked, done
):
    nq, faces = trace.shape[0], trace.shape[2]
    halo = up.shape[2]
    turned[...] = jnp.zeros_like(turned)
    turned[0:nq, :] = trace[:, 0, :]
    turned[HALF : HALF + nq, :] = trace[:, 1, :]
    rows[0:PAD, :] = jnp.zeros((PAD, LANES), F32)
    for first in range(0, faces, LANES):
        rows[PAD + first : PAD + first + LANES, :] = turned[:, first : first + LANES].T
    table_copy = begin(rows, table, done.at[0])
    gather_rows(DIRS * halo, halo_list, rows, picked)
    place_parcels(picked, halo, down, mid, up)
    table_copy.wait()


def sources_kernel(
    parts_in, elem_face,
    own_sum, up, mid, down,
    own, parts, sums0, sums1, sums2, sums3, sums4, sums5, sums6, sums7, ghosts, done,
):
    faces = own.shape[0]
    halo = up.shape[2]
    elems = parts.shape[1]
    parts_copy = begin(parts_in, parts, done.at[1])
    sums = (sums0, sums1, sums2, sums3, sums4, sums5, sums6, sums7)
    for total in sums:
        total[...] = jnp.zeros_like(total)
    parts_copy.wait()
    near = elems // 2

    def add_some(step, carry):
        for extra in range(4):
            elem = step * 4 + extra
            places = [
                (corner, elem + part * near) for corner in range(4) for part in range(2)
            ]
            slots = [elem_face[corner * elems + at] for corner, at in places]
            before = [total[pl.ds(slot, 1), :] for total, slot in zip(sums, slots)]
            values = [parts[corner, pl.ds(at, 1), :] for corner, at in places]
            for number, total in enumerate(sums):
                total[pl.ds(slots[number], 1), :] = before[number] + values[number]
        return carry

    lax.fori_loop(0, near // 4, add_some, 0)

    def summed(first, size):
        rows = [total[first : first + size, :] for total in sums]
        while len(rows) > 1:
            rows = [rows[k] + rows[k + 1] for k in range(0, len(rows), 2)]
        return rows[0]

    own[...] = summed(0, faces)
    own_copy = begin(own, own_sum, done.at[0])
    ghosts[...] = summed(faces, DIRS * halo)
    place_parcels(ghosts, halo, up, mid, down)
    own_copy.wait()


def halves(real, real_moved, imag, imag_moved, fill):
    high, rest = split(
        jnp.concatenate([real - imag_moved, fill, imag + real_moved, fill], axis=0)
    )
    return jnp.concatenate(
        [
            jnp.concatenate([high, high], axis=1),
            jnp.concatenate([rest, jnp.zeros_like(rest)], axis=1),
        ],
        axis=0,
    )


def operators_kernel(
    vol, flag, stretch, recon_op, cond_op, skel_op, lift_op,
    recon0, recon1, parts_out, skeleton, lifting,
    scaled, recon, cond, parts, done,
):
    nv, elems = vol.shape[1], vol.shape[2]
    nq = skel_op.shape[1]
    cond[...] = jnp.zeros_like(cond)
    for corner in range(4):
        real, imag = cond_op[corner, :, 0, :], cond_op[corner, :, 1, :]
        low = corner * LANES
        cond[low : low + nq, 0:nv] = real
        cond[low : low + nq, LANES : LANES + nv] = -imag
        cond[low + HALF : low + HALF + nq, 0:nv] = imag
        cond[low + HALF : low + HALF + nq, LANES : LANES + nv] = real
    scaled_volume(vol, flag, stretch, scaled)
    cond_high, cond_rest = split(cond[...])
    sent = []
    for first in range(0, elems, LANES):
        stop = first + LANES
        columns = jnp.concatenate(
            [scaled[0:LANES, first:stop].T, scaled[LANES : 2 * LANES, first:stop].T], axis=1
        )
        high, rest = split(columns)
        product = dot(high, cond_high, 1, 1) + dot(rest, cond_high, 1, 1) + dot(high, cond_rest, 1, 1)
        for corner in range(4):
            parts[corner, first:stop, :] = product[:, corner * LANES : (corner + 1) * LANES]
        sent.append(
            begin(
                parts.at[:, pl.ds(first, LANES), :],
                parts_out.at[:, pl.ds(first, LANES), :],
                done.at[first // LANES],
            )
        )
    for block in range(skel_op.shape[0]):
        low = block * 2 * ROWS
        skeleton[low : low + 2 * ROWS, :] = halves(
            *half_rolled(skel_op[block, :, 0, :], nq),
            *half_rolled(skel_op[block, :, 1, :], nq),
            jnp.zeros((HALF - nq, LANES), F32),
        )
    for corner in range(4):
        low = corner * 4 * LANES
        wide = []
        for part in range(2):
            block = jnp.concatenate(
                [lift_op[corner, :, part, :], jnp.zeros((nq, LANES - nv), F32)], axis=1
            )
            block = jnp.concatenate([block, jnp.zeros((LANES - nq, LANES), F32)], axis=0).T
            wide += [block, pltpu.roll(block, HALF, 1)]
        high, rest = split(jnp.concatenate([wide[0] - wide[3], wide[2] + wide[1]], axis=0))
        lifting[low : low + 2 * LANES, 0:LANES] = high
        lifting[low : low + 2 * LANES, LANES : 2 * LANES] = high
        lifting[low + 2 * LANES : low + 4 * LANES, 0:LANES] = rest
        lifting[low + 2 * LANES : low + 4 * LANES, LANES : 2 * LANES] = jnp.zeros_like(rest)
    recon[...] = jnp.zeros_like(recon)
    recon[0:nv, 0:nv] = recon_op[0]
    recon[0:nv, LANES : LANES + nv] = -recon_op[1]
    recon[LANES : LANES + nv, 0:nv] = recon_op[1]
    recon[LANES : LANES + nv, LANES : LANES + nv] = recon_op[0]
    high, rest = split(recon[...])
    size = 256
    part = recon0.shape[2]
    for first in range(0, elems, size):
        wanted, fine = split(scaled[:, first : first + size])
        product = dot(high, wanted) + dot(high, fine) + dot(rest, wanted)
        target = recon0 if first < part else recon1
        at = first % part
        target[0, :, at : at + size] = product[0:nv]
        target[1, :, at : at + size] = product[LANES : LANES + nv]
    for copy in sent:
        copy.wait()


def skeleton_tile(matrix, block_coef, slots, picked, first, size):
    real_sum = jnp.zeros((HALF, size), F32)
    imag_sum = jnp.zeros((HALF, size), F32)
    for block in range(block_coef.shape[0]):
        if block == 0:
            rows = slots[pl.ds(PAD + first, size), :]
        else:
            rows = picked[(block - 1) * size : block * size, :]
        high, rest = split(rows)
        low = block * 2 * ROWS
        product = dot(
            matrix[low : low + 2 * ROWS, :], jnp.concatenate([high, rest], axis=1), 1, 1
        )
        real = product[0:HALF] + product[ROWS : ROWS + HALF]
        imag = product[HALF:ROWS] + product[ROWS + HALF : 2 * ROWS]
        coef_real = block_coef[block, 0:1, pl.ds(first, size)]
        coef_imag = block_coef[block, 1:2, pl.ds(first, size)]
        real_sum = real_sum + (coef_real * real - coef_imag * imag)
        imag_sum = imag_sum + (coef_real * imag + coef_imag * real)
    return real_sum, imag_sum


def skeleton_loop(matrix, block_coef, adjacency, slots, picked, use, carry):
    tile = TILE
    faces = block_coef.shape[2]
    neighbours = block_coef.shape[0] - 1
    steps = faces // tile

    def fetch(step, target):
        for neighbour in range(neighbours):
            first = neighbour * faces + step * tile
            for extra in range(tile):
                row = adjacency[first + extra]
                at = neighbour * tile + extra
                target[at : at + 1, :] = slots[pl.ds(row + PAD, 1), :]

    def compute(step, source, carry):
        first = pl.multiple_of(step * tile, tile)
        real, imag = skeleton_tile(matrix, block_coef, slots, source, first, tile)
        return use(carry, first, real, imag)

    for neighbour in range(neighbours):
        gather_rows(tile, adjacency, slots, picked[0], neighbour * faces, neighbour * tile)

    def pair(number, carry):
        step = 2 * number
        fetch(step + 1, picked[1])
        carry = compute(step, picked[0], carry)
        fetch(step + 2, picked[0])
        return compute(step + 1, picked[1], carry)

    carry = lax.fori_loop(0, steps // 2 - 1, pair, carry)
    fetch(steps - 1, picked[1])
    carry = compute(steps - 2, picked[0], carry)
    return compute(steps - 1, picked[1], carry)


def join_kernel(up, mid, down, right, left, done):
    moves = [(down, 2, right, 0), (mid, 1, right, 1), (up, 2, right, 2)]
    moves += [(down, 0, left, 0), (mid, 0, left, 1), (up, 0, left, 2)]
    copies = [
        begin(source.at[place], target.at[to], done.at[number])
        for number, (source, place, target, to) in enumerate(moves)
    ]
    for copy in copies:
        copy.wait()


def ghost_places(up, down, right, left):
    return (
        left.at[0], down.at[1], right.at[0], left.at[1],
        right.at[1], left.at[2], up.at[1], right.at[2],
    )


def apply_kernel(
    table, own_sum, up, down, right, left, matrix, block_coef, adjacency,
    slots_out, rest_out,
    slots, own, rest, arrived, picked0, picked1, done,
):
    faces = own.shape[0]
    halo = arrived.shape[2]
    table_copy = begin(table, slots.at[pl.ds(0, PAD + faces)], done.at[0])
    copies = [
        begin(place, arrived.at[direction], done.at[3 + direction])
        for direction, place in enumerate(ghost_places(up, down, right, left))
    ]
    own_copy = begin(own_sum, own, done.at[1])
    for direction in range(DIRS):
        copies[direction].wait()
        first = PAD + faces + direction * halo
        slots[first : first + halo, :] = rows_of(arrived[direction])
    table_copy.wait()
    slots_copy = begin(slots, slots_out, done.at[2])
    own_copy.wait()

    def use(carry, first, real, imag):
        applied = rows_of(jnp.concatenate([real, imag], axis=0))
        rest[pl.ds(first, TILE), :] = own[pl.ds(first, TILE), :] - applied
        return carry

    skeleton_loop(matrix, block_coef, adjacency, slots, (picked0, picked1), use, 0)
    begin(rest, rest_out, done.at[0]).wait()
    slots_copy.wait()


def residual_kernel(
    rest, up, down, right, left, halo_list,
    rest_table, res_up, res_mid, res_down,
    returned, picked, back, sums0, sums1, sums2, sums3, sums4, sums5, sums6, sums7, done,
):
    faces = rest.shape[0]
    halo = returned.shape[2]
    rest_copy = begin(rest, sums0.at[pl.ds(PAD, faces)], done.at[0])
    places = (
        left.at[2], up.at[1], right.at[2], left.at[1],
        right.at[1], left.at[0], down.at[1], right.at[0],
    )
    copies = [
        begin(place, returned.at[direction], done.at[1 + direction])
        for direction, place in enumerate(places)
    ]
    sums0[0:PAD, :] = jnp.zeros((PAD, LANES), F32)
    others = (sums1, sums2, sums3, sums4, sums5, sums6, sums7)
    for total in others:
        total[...] = jnp.zeros_like(total)
    for direction in range(DIRS):
        copies[direction].wait()
        back[direction] = rows_of(returned[direction])
    rest_copy.wait()
    sums = (sums0,) + others

    def add_some(step, carry):
        for extra in range(4):
            entry = step * 4 + extra
            places = [halo_list[direction * halo + entry] + PAD for direction in range(DIRS)]
            before = [total[pl.ds(place, 1), :] for total, place in zip(sums, places)]
            values = [back[direction, pl.ds(entry, 1), :] for direction in range(DIRS)]
            for number, total in enumerate(sums):
                total[pl.ds(places[number], 1), :] = before[number] + values[number]
        return carry

    lax.fori_loop(0, halo // 4, add_some, 0)
    rest_table[...] = ((sums0[...] + sums1[...]) + (sums2[...] + sums3[...])) + (
        (sums4[...] + sums5[...]) + (sums6[...] + sums7[...])
    )
    rest_table[0:PAD, :] = jnp.zeros((PAD, LANES), F32)
    gather_rows(DIRS * halo, halo_list, rest_table, picked)
    place_parcels(picked, halo, res_down, res_mid, res_up)


def turn_kernel(rest_table, turned):
    for first in range(0, turned.shape[1], LANES):
        turned[:, first : first + LANES] = parcel_of(
            rest_table[PAD + first : PAD + first + LANES, :]
        )


def lifted_loop(matrix, elem_face, start, count, elems, slots, picked, use):
    size = LIFT

    def fetch(step, target):
        for corner in range(4):
            first = corner * count + start + step * size
            for extra in range(size):
                row = elem_face[first + extra]
                at = corner * size + extra
                target[at : at + 1, :] = slots[pl.ds(row + PAD, 1), :]

    def compute(step, rows):
        total = jnp.zeros((2 * LANES, size), F32)
        for corner in range(4):
            high, rest = split(rows[corner * size : (corner + 1) * size, :])
            at = corner * 4 * LANES
            product = dot(
                matrix[at : at + 4 * LANES, :], jnp.concatenate([high, rest], axis=1), 1, 1
            )
            total = total + (product[0 : 2 * LANES] + product[2 * LANES : 4 * LANES])
        use(step * size, total)

    steps = elems // size
    fetch(0, picked[0])
    for step in range(steps):
        if step + 1 < steps:
            fetch(step + 1, picked[(step + 1) % 2])
        compute(step, picked[step % 2])


def base_kernel(
    start, count, slots_in, recon, matrix, elem_face, base, slots, picked0, picked1, done
):
    nv, elems = base.shape[1], base.shape[2]
    begin(slots_in, slots, done.at[0]).wait()

    def use(first, product):
        stop = first + LIFT
        base[0, :, first:stop] = recon[0, :, first:stop] - product[0:nv]
        base[1, :, first:stop] = recon[1, :, first:stop] - product[LANES : LANES + nv]

    lifted_loop(matrix, elem_face, start, count, elems, slots, (picked0, picked1), use)


def lift_kernel(slots_in, matrix, elem_face, lifted, slots, picked0, picked1, done):
    nv, elems = lifted.shape[1], lifted.shape[2]
    begin(slots_in, slots, done.at[0]).wait()

    def use(first, product):
        stop = first + LIFT
        lifted[0, :, first:stop] = product[0:nv]
        lifted[1, :, first:stop] = product[LANES : LANES + nv]

    lifted_loop(matrix, elem_face, 0, elems, elems, slots, (picked0, picked1), use)


def image_kernel(
    rest_table, turned, up, down, right, left, matrix, block_coef, adjacency,
    slots_out, partial,
    slots, arrived, picked0, picked1, done,
):
    faces = turned.shape[1]
    halo = arrived.shape[2]
    table_copy = begin(rest_table, slots.at[pl.ds(0, PAD + faces)], done.at[0])
    copies = [
        begin(place, arrived.at[direction], done.at[3 + direction])
        for direction, place in enumerate(ghost_places(up, down, right, left))
    ]
    for direction in range(DIRS):
        copies[direction].wait()
        first = PAD + faces + direction * halo
        slots[first : first + halo, :] = rows_of(arrived[direction])
    table_copy.wait()
    slots_copy = begin(slots, slots_out, done.at[2])

    def use(carry, first, real, imag):
        rest_real = turned[0:HALF, pl.ds(first, TILE)]
        rest_imag = turned[HALF:ROWS, pl.ds(first, TILE)]
        return (
            carry[0] + (real * rest_real + imag * rest_imag),
            carry[1] + (real * rest_imag - imag * rest_real),
            carry[2] + (real * real + imag * imag),
        )

    zero = jnp.zeros((HALF, TILE), F32)
    totals = skeleton_loop(
        matrix, block_coef, adjacency, slots, (picked0, picked1), use, (zero, zero, zero)
    )
    lane = lax.broadcasted_iota(jnp.int32, (1, LANES), 1)
    line = jnp.zeros((1, LANES), F32)
    for place in range(3):
        line = line + jnp.where(lane == place, jnp.sum(totals[place]), 0.0)
    partial[...] = jnp.broadcast_to(line, partial.shape)
    slots_copy.wait()


def finish_kernel(gathered, trace, turned, base0, base1, lifted, trace_out, volume_out):
    nq = trace.shape[0]
    line = jnp.sum(gathered[...], axis=0, keepdims=True)
    lane = lax.broadcasted_iota(jnp.int32, (1, LANES), 1)
    entry = [
        jnp.sum(jnp.where(lane == place, line, 0.0), axis=1, keepdims=True)
        for place in range(3)
    ]
    step_real = entry[0] / entry[2]
    step_imag = entry[1] / entry[2]
    first = 0
    for base in (base0, base1):
        stop = first + base.shape[2]
        real, imag = lifted[0, :, first:stop], lifted[1, :, first:stop]
        volume_out[0, :, first:stop] = base[0] - (step_real * real - step_imag * imag)
        volume_out[1, :, first:stop] = base[1] - (step_real * imag + step_imag * real)
        first = stop
    rest_real = turned[0:nq, :]
    rest_imag = turned[HALF : HALF + nq, :]
    trace_out[:, 0, :] = trace[:, 0, :] + (step_real * rest_real - step_imag * rest_imag)
    trace_out[:, 1, :] = trace[:, 1, :] + (step_real * rest_imag + step_imag * rest_real)


SPACES = {
    "v": pltpu.MemorySpace.VMEM,
    "s": pltpu.MemorySpace.SMEM,
    "a": pl.ANY,
    "h": pltpu.HBM,
    "V": pltpu.MemorySpace.VMEM,
    "B": pltpu.MemorySpace.VMEM,
}


def call(kernel, name, args, out_shapes, spaces, scratch, limit, semaphores=0, time=1):
    specs = [pl.BlockSpec(memory_space=SPACES[letter]) for letter in spaces]
    shapes = [pltpu.VMEM(shape, kind) for shape, kind in scratch]
    if semaphores:
        shapes.append(pltpu.SemaphoreType.DMA((semaphores,)))
    args = [
        pltpu.with_memory_space_constraint(arg, pltpu.HBM) if letter in "hVB" else arg
        for arg, letter in zip(args, spaces)
    ]
    return pl.pallas_call(
        kernel,
        name=name,
        out_shape=[
            pltpu.HBM(shape, BF16 if letter == "B" else F32)
            if letter in "hVB"
            else jax.ShapeDtypeStruct(shape, F32)
            for shape, letter in zip(out_shapes, spaces[len(args) :])
        ],
        in_specs=specs[: len(args)],
        out_specs=specs[len(args) :],
        scratch_shapes=shapes,
        compiler_params=pltpu.CompilerParams(vmem_limit_bytes=limit * MIB),
        cost_estimate=pl.CostEstimate(
            flops=0, bytes_accessed=3300000 * time, transcendentals=0
        ),
    )(*args)


def from_behind(block, axis, distance):
    devices = range(lax.axis_size(axis))
    route = [(i - distance, i) for i in devices if i - distance in devices]
    return lax.ppermute(block, axis, route)


def everywhere(lines, axis):
    return lax.all_to_all(lines, axis, 0, 0)


def local(
    vol_rhs, trace_in, pml_flag, stretch, cond_op, skel_op, block_coef, recon_op, lift_op,
    elem_face, adjacency, halo_list,
):
    nv, elems = vol_rhs.shape[1], vol_rhs.shape[2]
    faces = trace_in.shape[2]
    halo = halo_list.shape[1]
    blocks = skel_op.shape[0]
    neighbours = adjacency.shape[0]
    slots = faces + DIRS * halo
    elem_face = elem_face.reshape(-1)
    adjacency = adjacency.reshape(-1)
    halo_list = halo_list.reshape(-1)
    flag = pml_flag.reshape(1, elems)
    tilt = stretch.reshape(1, elems)
    parcels = [(3, ROWS, halo), (2, ROWS, halo), (3, ROWS, halo)]

    def exchange(up, mid, down, sign, beside):
        up = from_behind(up, "gx", 1)
        down = from_behind(down, "gx", -1)
        up, down, beside = lax.optimization_barrier((up, down, beside))
        right, left = call(
            join_kernel, "join", (up, mid, down), [up.shape, up.shape], "aaa" + "vv", [], 2, 6
        )
        right = from_behind(right, "gy", sign)
        left = from_behind(left, "gy", -sign)
        return (up, down, right, left), beside

    trace_pairs = jnp.transpose(trace_in, (1, 0, 2))
    table, *outgoing = call(
        traces_kernel,
        "traces",
        (trace_pairs, halo_list),
        [(PAD + faces, LANES)] + parcels,
        "Vs" + "hvvv",
        [((PAD + faces, LANES), F32), ((LANES, faces), F32), ((DIRS * halo, LANES), F32)],
        8,
        1,
        4,
    )
    near = elems // 2
    operators = call(
        operators_kernel,
        "operators",
        (
            vol_rhs, flag, tilt, recon_op, jnp.transpose(cond_op, (0, 2, 1, 3)),
            jnp.transpose(skel_op, (0, 2, 1, 3)), jnp.transpose(lift_op, (0, 3, 1, 2)),
        ),
        [(2, nv, near), (2, nv, elems - near)]
        + [(4, elems, LANES)]
        + [(blocks * 2 * ROWS, 2 * LANES), (4 * 4 * LANES, 2 * LANES)],
        "VVVVVVV" + "VVhBB",
        [
            ((2 * LANES, elems), F32),
            ((2 * LANES, 2 * LANES), F32),
            ((4 * LANES, 2 * LANES), F32),
            ((4, elems, LANES), F32),
        ],
        18,
        elems // LANES,
        8,
    )
    arrived, operators = exchange(*outgoing, 1, operators)
    recon0, recon1, parts, skeleton, lifting = operators
    own_sum, *outgoing = call(
        sources_kernel,
        "sources",
        (parts, elem_face),
        [(faces, LANES)] + parcels,
        "hs" + "hvvv",
        [
            ((faces, LANES), F32),
            ((4, elems, LANES), F32),
        ]
        + [((slots, LANES), F32)] * 8
        + [((DIRS * halo, LANES), F32)],
        30,
        2,
        7,
    )
    slots_trace, rest = call(
        apply_kernel,
        "apply",
        (table, own_sum, *arrived, skeleton, block_coef, adjacency),
        [(PAD + slots, LANES), (faces, LANES)],
        "hhaaaaBVs" + "hh",
        [
            ((PAD + slots, LANES), F32),
            ((faces, LANES), F32),
            ((faces, LANES), F32),
            ((DIRS, ROWS, halo), F32),
            ((neighbours * TILE, LANES), F32),
            ((neighbours * TILE, LANES), F32),
        ],
        16,
        3 + DIRS,
        16,
    )
    returned, (slots_trace, rest) = exchange(*outgoing, -1, (slots_trace, rest))

    def base_part(start, recon):
        return call(
            functools.partial(base_kernel, start, elems),
            "base",
            (slots_trace, recon, lifting, elem_face),
            [recon.shape],
            "hVBs" + "V",
            [((PAD + slots, LANES), F32)] + [((4 * LIFT, LANES), F32)] * 2,
            10,
            1,
            5,
        )[0]

    base0 = base_part(0, recon0)
    *returned, base0 = lax.optimization_barrier((*returned, base0))
    rest_table, *outgoing = call(
        residual_kernel,
        "residual",
        (rest, *returned, halo_list),
        [(PAD + faces, LANES)] + parcels,
        "haaaas" + "Vvvv",
        [
            ((DIRS, ROWS, halo), F32),
            ((DIRS * halo, LANES), F32),
            ((DIRS, halo, LANES), F32),
        ]
        + [((PAD + faces, LANES), F32)] * 8,
        16,
        1 + DIRS,
        8,
    )
    base1 = base_part(near, recon1)
    arrived, base1 = exchange(*outgoing, 1, base1)
    (turned,) = call(turn_kernel, "turn", (rest_table,), [(ROWS, faces)], "VV", [], 4)
    across, along = lax.axis_size("gx"), lax.axis_size("gy")
    slots_rest, partial = call(
        image_kernel,
        "image",
        (rest_table, turned, *arrived, skeleton, block_coef, adjacency),
        [(PAD + slots, LANES), (along, LANES)],
        "hVaaaaBVs" + "hv",
        [
            ((PAD + slots, LANES), F32),
            ((DIRS, ROWS, halo), F32),
            ((neighbours * TILE, LANES), F32),
            ((neighbours * TILE, LANES), F32),
        ],
        16,
        3 + DIRS,
        16,
    )
    (lifted,) = call(
        lift_kernel,
        "lift",
        (slots_rest, lifting, elem_face),
        [vol_rhs.shape],
        "hBs" + "V",
        [((PAD + slots, LANES), F32)] + [((4 * LIFT, LANES), F32)] * 2,
        12,
        1,
        7,
    )
    lines, lifted = lax.optimization_barrier((everywhere(partial, "gy"), lifted))
    lines = jnp.sum(lines, axis=0, keepdims=True)
    gathered = everywhere(jnp.broadcast_to(lines, (across, LANES)), "gx")
    trace_pairs, volume_out = call(
        finish_kernel,
        "finish",
        (gathered, trace_pairs, turned, base0, base1, lifted),
        [trace_pairs.shape, vol_rhs.shape],
        "vvvvvv" + "VV",
        [],
        8,
    )
    trace_out = jnp.transpose(trace_pairs, (1, 0, 2))
    return trace_out, volume_out


def solution(mesh):
    split_last = ("gx", "gy")
    in_specs = (
        P(None, None, split_last),
        P(None, None, split_last),
        P(split_last),
        P(split_last),
        P(),
        P(),
        P(None, None, split_last),
        P(),
        P(),
        P(None, split_last),
        P(None, split_last),
        P(None, split_last),
    )
    out_specs = (P(None, None, split_last), P(None, None, split_last))
    return jax.shard_map(
        local, mesh=mesh, in_specs=in_specs, out_specs=out_specs, check_vma=False
    )
```

```python
import functools

import jax
import jax.numpy as jnp
from jax import lax
from jax.experimental import pallas as pl
from jax.experimental.pallas import tpu as pltpu
from jax.sharding import PartitionSpec as P

F32 = jnp.float32
BF16 = jnp.bfloat16
HALF = 40
ROWS = 2 * HALF
LANES = 128
PAD = 8
DIRS = 8
UNROLL = 128
TILE = 256
LIFT = 256
MIB = 1 << 20


def split(values):
    high = values.astype(BF16)
    return high, (values - high.astype(F32)).astype(BF16)


def dot(left, right, left_dim=1, right_dim=0):
    return lax.dot_general(
        left, right, (((left_dim,), (right_dim,)), ((), ())), preferred_element_type=F32
    )


def half_rolled(block, height):
    wide = jnp.concatenate(
        [block, jnp.zeros((height, LANES - block.shape[1]), F32)], axis=1
    )
    return wide, pltpu.roll(wide, HALF, 1)


def gather_rows(count, indices, source, target, start=0, base=0):
    def some(step, carry):
        first = step * UNROLL
        for extra in range(UNROLL):
            row = indices[start + first + extra]
            target[pl.ds(base + first + extra, 1), :] = source[pl.ds(row + PAD, 1), :]
        return carry

    lax.fori_loop(0, count // UNROLL, some, 0)


def begin(source, target, semaphore):
    copy = pltpu.make_async_copy(source, target, semaphore)
    copy.start()
    return copy


def parcel_of(rows):
    return rows.T[:ROWS]


def rows_of(parcel):
    halo = parcel.shape[1]
    return jnp.concatenate([parcel, jnp.zeros((LANES - ROWS, halo), F32)], axis=0).T


def scaled_volume(vol, flag, stretch, scaled):
    nv = vol.shape[1]
    tilt = flag[...].astype(F32) * stretch[...]
    real, imag = vol[0], vol[1]
    fill = jnp.zeros((LANES - nv, vol.shape[2]), F32)
    scaled[0:nv, :] = real - tilt * imag
    scaled[nv:LANES, :] = fill
    scaled[LANES : LANES + nv, :] = imag + tilt * real
    scaled[LANES + nv : 2 * LANES, :] = fill


def place_parcels(picked, halo, lower, middle, upper):
    for direction in range(DIRS):
        parcel = parcel_of(picked[direction * halo : (direction + 1) * halo, :])
        if direction < 3:
            lower[direction] = parcel
        elif direction < 5:
            middle[direction - 3] = parcel
        else:
            upper[direction - 5] = parcel


def prepare_kernel(
    trace, vol, flag, stretch, cond_op, halo_list, elem_face,
    table, own_sum, up, mid, down,
    rows, turned, picked, own, scaled, cond, parts,
    sums0, sums1, sums2, sums3, sums4, sums5, sums6, sums7, done,
):
    nq, faces = trace.shape[0], trace.shape[2]
    nv, elems = vol.shape[1], vol.shape[2]
    halo = up.shape[2]
    turned[...] = jnp.zeros_like(turned)
    turned[0:nq, :] = trace[:, 0, :]
    turned[HALF : HALF + nq, :] = trace[:, 1, :]
    rows[0:PAD, :] = jnp.zeros((PAD, LANES), F32)
    for first in range(0, faces, LANES):
        rows[PAD + first : PAD + first + LANES, :] = turned[:, first : first + LANES].T
    table_copy = begin(rows, table, done.at[0])
    cond[...] = jnp.zeros_like(cond)
    for corner in range(4):
        real, imag = cond_op[corner, :, 0, :], cond_op[corner, :, 1, :]
        low = corner * LANES
        cond[low : low + nq, 0:nv] = real
        cond[low : low + nq, LANES : LANES + nv] = -imag
        cond[low + HALF : low + HALF + nq, 0:nv] = imag
        cond[low + HALF : low + HALF + nq, LANES : LANES + nv] = real
    scaled_volume(vol, flag, stretch, scaled)
    cond_high, cond_rest = split(cond[...])
    for first in range(0, elems, LANES):
        stop = first + LANES
        columns = jnp.concatenate(
            [scaled[0:LANES, first:stop].T, scaled[LANES : 2 * LANES, first:stop].T], axis=1
        )
        high, rest = split(columns)
        product = dot(high, cond_high, 1, 1) + dot(rest, cond_high, 1, 1) + dot(high, cond_rest, 1, 1)
        for corner in range(4):
            parts[corner, first:stop, :] = product[:, corner * LANES : (corner + 1) * LANES]
    sums = (sums0, sums1, sums2, sums3, sums4, sums5, sums6, sums7)
    for total in sums:
        total[...] = jnp.zeros_like(total)
    near = elems // 2

    def add_some(step, carry):
        for extra in range(4):
            elem = step * 4 + extra
            places = [
                (corner, elem + part * near) for corner in range(4) for part in range(2)
            ]
            slots = [elem_face[corner * elems + at] for corner, at in places]
            before = [total[pl.ds(slot, 1), :] for total, slot in zip(sums, slots)]
            values = [parts[corner, pl.ds(at, 1), :] for corner, at in places]
            for number, total in enumerate(sums):
                total[pl.ds(slots[number], 1), :] = before[number] + values[number]
        return carry

    lax.fori_loop(0, near // 4, add_some, 0)

    def summed(first, size):
        lines = [total[first : first + size, :] for total in sums]
        while len(lines) > 1:
            lines = [lines[k] + lines[k + 1] for k in range(0, len(lines), 2)]
        return lines[0]

    own[...] = summed(0, faces)
    own_copy = begin(own, own_sum, done.at[1])
    gather_rows(DIRS * halo, halo_list, rows, picked)
    for direction in range(DIRS):
        parcel = parcel_of(picked[direction * halo : (direction + 1) * halo, :])
        back = parcel_of(summed(faces + direction * halo, halo))
        if direction < 3:
            down[direction] = parcel
            up[3 + direction] = back
        elif direction < 5:
            mid[direction - 3] = parcel
            mid[direction - 1] = back
        else:
            up[direction - 5] = parcel
            down[direction - 2] = back
    table_copy.wait()
    own_copy.wait()


def halves(real, real_moved, imag, imag_moved, fill):
    high, rest = split(
        jnp.concatenate([real - imag_moved, fill, imag + real_moved, fill], axis=0)
    )
    return jnp.concatenate(
        [
            jnp.concatenate([high, high], axis=1),
            jnp.concatenate([rest, jnp.zeros_like(rest)], axis=1),
        ],
        axis=0,
    )


def operators_kernel(
    vol, flag, stretch, recon_op, skel_op, lift_op, recon_out, skeleton, lifting, scaled, recon
):
    nv, elems = vol.shape[1], vol.shape[2]
    nq = skel_op.shape[1]
    scaled_volume(vol, flag, stretch, scaled)
    for block in range(skel_op.shape[0]):
        low = block * 2 * ROWS
        skeleton[low : low + 2 * ROWS, :] = halves(
            *half_rolled(skel_op[block, :, 0, :], nq),
            *half_rolled(skel_op[block, :, 1, :], nq),
            jnp.zeros((HALF - nq, LANES), F32),
        )
    for corner in range(4):
        low = corner * 4 * LANES
        wide = []
        for part in range(2):
            block = jnp.concatenate(
                [lift_op[corner, :, part, :], jnp.zeros((nq, LANES - nv), F32)], axis=1
            )
            block = jnp.concatenate([block, jnp.zeros((LANES - nq, LANES), F32)], axis=0).T
            wide += [block, pltpu.roll(block, HALF, 1)]
        high, rest = split(jnp.concatenate([wide[0] - wide[3], wide[2] + wide[1]], axis=0))
        lifting[low : low + 2 * LANES, 0:LANES] = high
        lifting[low : low + 2 * LANES, LANES : 2 * LANES] = high
        lifting[low + 2 * LANES : low + 4 * LANES, 0:LANES] = rest
        lifting[low + 2 * LANES : low + 4 * LANES, LANES : 2 * LANES] = jnp.zeros_like(rest)
    recon[...] = jnp.zeros_like(recon)
    recon[0:nv, 0:nv] = recon_op[0]
    recon[0:nv, LANES : LANES + nv] = -recon_op[1]
    recon[LANES : LANES + nv, 0:nv] = recon_op[1]
    recon[LANES : LANES + nv, LANES : LANES + nv] = recon_op[0]
    high, rest = split(recon[...])
    size = 256
    for first in range(0, elems, size):
        stop = first + size
        wanted, fine = split(scaled[:, first:stop])
        product = dot(high, wanted) + dot(high, fine) + dot(rest, wanted)
        recon_out[0, :, first:stop] = product[0:nv]
        recon_out[1, :, first:stop] = product[LANES : LANES + nv]


def skeleton_tile(matrix, block_coef, slots, picked, first, size):
    real_sum = jnp.zeros((HALF, size), F32)
    imag_sum = jnp.zeros((HALF, size), F32)
    for block in range(block_coef.shape[0]):
        if block == 0:
            rows = slots[pl.ds(PAD + first, size), :]
        else:
            rows = picked[(block - 1) * size : block * size, :]
        high, rest = split(rows)
        low = block * 2 * ROWS
        product = dot(
            matrix[low : low + 2 * ROWS, :], jnp.concatenate([high, rest], axis=1), 1, 1
        )
        real = product[0:HALF] + product[ROWS : ROWS + HALF]
        imag = product[HALF:ROWS] + product[ROWS + HALF : 2 * ROWS]
        coef_real = block_coef[block, 0:1, pl.ds(first, size)]
        coef_imag = block_coef[block, 1:2, pl.ds(first, size)]
        real_sum = real_sum + (coef_real * real - coef_imag * imag)
        imag_sum = imag_sum + (coef_real * imag + coef_imag * real)
    return real_sum, imag_sum


def skeleton_loop(matrix, block_coef, adjacency, slots, picked, use, carry):
    tile = TILE
    faces = block_coef.shape[2]
    neighbours = block_coef.shape[0] - 1
    steps = faces // tile

    def fetch(step, target):
        for neighbour in range(neighbours):
            first = neighbour * faces + step * tile
            for extra in range(tile):
                row = adjacency[first + extra]
                at = neighbour * tile + extra
                target[at : at + 1, :] = slots[pl.ds(row + PAD, 1), :]

    def compute(step, source, carry):
        first = pl.multiple_of(step * tile, tile)
        real, imag = skeleton_tile(matrix, block_coef, slots, source, first, tile)
        return use(carry, first, real, imag)

    for neighbour in range(neighbours):
        gather_rows(tile, adjacency, slots, picked[0], neighbour * faces, neighbour * tile)

    def pair(number, carry):
        step = 2 * number
        fetch(step + 1, picked[1])
        carry = compute(step, picked[0], carry)
        fetch(step + 2, picked[0])
        return compute(step + 1, picked[1], carry)

    carry = lax.fori_loop(0, steps // 2 - 1, pair, carry)
    fetch(steps - 1, picked[1])
    carry = compute(steps - 2, picked[0], carry)
    return compute(steps - 1, picked[1], carry)


def join_kernel(up, mid, down, right, left, done):
    moves = [(down, 2, right, 0), (mid, 1, right, 1), (up, 2, right, 2)]
    moves += [(down, 0, left, 0), (mid, 0, left, 1), (up, 0, left, 2)]
    if up.shape[0] == 6:
        moves += [(up, 3, right, 3), (mid, 2, right, 4), (down, 3, right, 5)]
        moves += [(up, 5, left, 3), (mid, 3, left, 4), (down, 5, left, 5)]
    copies = [
        begin(source.at[place], target.at[to], done.at[number])
        for number, (source, place, target, to) in enumerate(moves)
    ]
    for copy in copies:
        copy.wait()


def ghost_places(up, down, right, left):
    return (
        left.at[0], down.at[1], right.at[0], left.at[1],
        right.at[1], left.at[2], up.at[1], right.at[2],
    )


def apply_kernel(
    table, own_sum, up, down, right, left, matrix, block_coef, adjacency,
    slots_out, rest_out,
    slots, own, rest, arrived, picked0, picked1, done,
):
    faces = own.shape[0]
    halo = arrived.shape[2]
    table_copy = begin(table, slots.at[pl.ds(0, PAD + faces)], done.at[0])
    copies = [
        begin(place, arrived.at[direction], done.at[3 + direction])
        for direction, place in enumerate(ghost_places(up, down, right, left))
    ]
    own_copy = begin(own_sum, own, done.at[1])
    for direction in range(DIRS):
        copies[direction].wait()
        first = PAD + faces + direction * halo
        slots[first : first + halo, :] = rows_of(arrived[direction])
    table_copy.wait()
    slots_copy = begin(slots, slots_out, done.at[2])
    own_copy.wait()

    def use(carry, first, real, imag):
        applied = rows_of(jnp.concatenate([real, imag], axis=0))
        rest[pl.ds(first, TILE), :] = own[pl.ds(first, TILE), :] - applied
        return carry

    skeleton_loop(matrix, block_coef, adjacency, slots, (picked0, picked1), use, 0)
    begin(rest, rest_out, done.at[0]).wait()
    slots_copy.wait()


def residual_kernel(
    rest, up, down, right, left, halo_list,
    rest_table, res_up, res_mid, res_down,
    returned, picked, back, sums0, sums1, sums2, sums3, sums4, sums5, sums6, sums7, done,
):
    faces = rest.shape[0]
    halo = returned.shape[2]
    rest_copy = begin(rest, sums0.at[pl.ds(PAD, faces)], done.at[0])
    places = (
        right.at[3], up.at[4], left.at[3], right.at[4],
        left.at[4], right.at[5], down.at[4], left.at[5],
    )
    copies = [
        begin(place, returned.at[direction], done.at[1 + direction])
        for direction, place in enumerate(places)
    ]
    sums0[0:PAD, :] = jnp.zeros((PAD, LANES), F32)
    others = (sums1, sums2, sums3, sums4, sums5, sums6, sums7)
    for total in others:
        total[...] = jnp.zeros_like(total)
    for direction in range(DIRS):
        copies[direction].wait()
        back[direction] = rows_of(returned[direction])
    rest_copy.wait()
    sums = (sums0,) + others

    def add_some(step, carry):
        for extra in range(4):
            entry = step * 4 + extra
            places = [halo_list[direction * halo + entry] + PAD for direction in range(DIRS)]
            before = [total[pl.ds(place, 1), :] for total, place in zip(sums, places)]
            values = [back[direction, pl.ds(entry, 1), :] for direction in range(DIRS)]
            for number, total in enumerate(sums):
                total[pl.ds(places[number], 1), :] = before[number] + values[number]
        return carry

    lax.fori_loop(0, halo // 4, add_some, 0)
    rest_table[...] = ((sums0[...] + sums1[...]) + (sums2[...] + sums3[...])) + (
        (sums4[...] + sums5[...]) + (sums6[...] + sums7[...])
    )
    rest_table[0:PAD, :] = jnp.zeros((PAD, LANES), F32)
    gather_rows(DIRS * halo, halo_list, rest_table, picked)
    place_parcels(picked, halo, res_down, res_mid, res_up)


def turn_kernel(rest_table, turned):
    for first in range(0, turned.shape[1], LANES):
        turned[:, first : first + LANES] = parcel_of(
            rest_table[PAD + first : PAD + first + LANES, :]
        )


def lifted_loop(matrix, elem_face, elems, slots, picked, use):
    size = LIFT

    def fetch(step, target):
        for corner in range(4):
            first = corner * elems + step * size
            for extra in range(size):
                row = elem_face[first + extra]
                at = corner * size + extra
                target[at : at + 1, :] = slots[pl.ds(row + PAD, 1), :]

    def compute(step, rows):
        total = jnp.zeros((2 * LANES, size), F32)
        for corner in range(4):
            high, rest = split(rows[corner * size : (corner + 1) * size, :])
            at = corner * 4 * LANES
            product = dot(
                matrix[at : at + 4 * LANES, :], jnp.concatenate([high, rest], axis=1), 1, 1
            )
            total = total + (product[0 : 2 * LANES] + product[2 * LANES : 4 * LANES])
        use(step * size, total)

    steps = elems // size
    fetch(0, picked[0])
    for step in range(steps):
        if step + 1 < steps:
            fetch(step + 1, picked[(step + 1) % 2])
        compute(step, picked[step % 2])


def base_kernel(
    slots_in, recon, matrix, elem_face, base, slots, picked0, picked1, done
):
    nv, elems = base.shape[1], base.shape[2]
    begin(slots_in, slots, done.at[0]).wait()

    def use(first, product):
        stop = first + LIFT
        base[0, :, first:stop] = recon[0, :, first:stop] - product[0:nv]
        base[1, :, first:stop] = recon[1, :, first:stop] - product[LANES : LANES + nv]

    lifted_loop(matrix, elem_face, elems, slots, (picked0, picked1), use)


def lift_kernel(slots_in, matrix, elem_face, lifted, slots, picked0, picked1, done):
    nv, elems = lifted.shape[1], lifted.shape[2]
    begin(slots_in, slots, done.at[0]).wait()

    def use(first, product):
        stop = first + LIFT
        lifted[0, :, first:stop] = product[0:nv]
        lifted[1, :, first:stop] = product[LANES : LANES + nv]

    lifted_loop(matrix, elem_face, elems, slots, (picked0, picked1), use)


def image_kernel(
    rest_table, turned, up, down, right, left, matrix, block_coef, adjacency,
    slots_out, partial,
    slots, arrived, picked0, picked1, done,
):
    faces = turned.shape[1]
    halo = arrived.shape[2]
    table_copy = begin(rest_table, slots.at[pl.ds(0, PAD + faces)], done.at[0])
    copies = [
        begin(place, arrived.at[direction], done.at[3 + direction])
        for direction, place in enumerate(ghost_places(up, down, right, left))
    ]
    for direction in range(DIRS):
        copies[direction].wait()
        first = PAD + faces + direction * halo
        slots[first : first + halo, :] = rows_of(arrived[direction])
    table_copy.wait()
    slots_copy = begin(slots, slots_out, done.at[2])

    def use(carry, first, real, imag):
        rest_real = turned[0:HALF, pl.ds(first, TILE)]
        rest_imag = turned[HALF:ROWS, pl.ds(first, TILE)]
        return (
            carry[0] + (real * rest_real + imag * rest_imag),
            carry[1] + (real * rest_imag - imag * rest_real),
            carry[2] + (real * real + imag * imag),
        )

    zero = jnp.zeros((HALF, TILE), F32)
    totals = skeleton_loop(
        matrix, block_coef, adjacency, slots, (picked0, picked1), use, (zero, zero, zero)
    )
    lane = lax.broadcasted_iota(jnp.int32, (1, LANES), 1)
    line = jnp.zeros((1, LANES), F32)
    for place in range(3):
        line = line + jnp.where(lane == place, jnp.sum(totals[place]), 0.0)
    partial[...] = jnp.broadcast_to(line, partial.shape)
    slots_copy.wait()


def finish_kernel(gathered, trace, turned, base, lifted, trace_out, volume_out):
    nq = trace.shape[0]
    line = jnp.sum(gathered[...], axis=0, keepdims=True)
    lane = lax.broadcasted_iota(jnp.int32, (1, LANES), 1)
    entry = [
        jnp.sum(jnp.where(lane == place, line, 0.0), axis=1, keepdims=True)
        for place in range(3)
    ]
    step_real = entry[0] / entry[2]
    step_imag = entry[1] / entry[2]
    volume_out[0] = base[0] - (step_real * lifted[0] - step_imag * lifted[1])
    volume_out[1] = base[1] - (step_real * lifted[1] + step_imag * lifted[0])
    rest_real = turned[0:nq, :]
    rest_imag = turned[HALF : HALF + nq, :]
    trace_out[:, 0, :] = trace[:, 0, :] + (step_real * rest_real - step_imag * rest_imag)
    trace_out[:, 1, :] = trace[:, 1, :] + (step_real * rest_imag + step_imag * rest_real)


SPACES = {
    "v": pltpu.MemorySpace.VMEM,
    "s": pltpu.MemorySpace.SMEM,
    "a": pl.ANY,
    "h": pltpu.HBM,
    "V": pltpu.MemorySpace.VMEM,
    "B": pltpu.MemorySpace.VMEM,
}


def call(kernel, name, args, out_shapes, spaces, scratch, limit, semaphores=0, time=1):
    specs = [pl.BlockSpec(memory_space=SPACES[letter]) for letter in spaces]
    shapes = [pltpu.VMEM(shape, kind) for shape, kind in scratch]
    if semaphores:
        shapes.append(pltpu.SemaphoreType.DMA((semaphores,)))
    args = [
        pltpu.with_memory_space_constraint(arg, pltpu.HBM) if letter in "hVB" else arg
        for arg, letter in zip(args, spaces)
    ]
    return pl.pallas_call(
        kernel,
        name=name,
        out_shape=[
            pltpu.HBM(shape, BF16 if letter == "B" else F32)
            if letter in "hVB"
            else jax.ShapeDtypeStruct(shape, F32)
            for shape, letter in zip(out_shapes, spaces[len(args) :])
        ],
        in_specs=specs[: len(args)],
        out_specs=specs[len(args) :],
        scratch_shapes=shapes,
        compiler_params=pltpu.CompilerParams(vmem_limit_bytes=limit * MIB),
        cost_estimate=pl.CostEstimate(
            flops=0, bytes_accessed=3300000 * time, transcendentals=0
        ),
    )(*args)


def from_behind(block, axis, distance):
    devices = range(lax.axis_size(axis))
    route = [(i - distance, i) for i in devices if i - distance in devices]
    return lax.ppermute(block, axis, route)


def everywhere(lines, axis):
    return lax.all_to_all(lines, axis, 0, 0)


def local(
    vol_rhs, trace_in, pml_flag, stretch, cond_op, skel_op, block_coef, recon_op, lift_op,
    elem_face, adjacency, halo_list,
):
    nv, elems = vol_rhs.shape[1], vol_rhs.shape[2]
    faces = trace_in.shape[2]
    halo = halo_list.shape[1]
    blocks = skel_op.shape[0]
    neighbours = adjacency.shape[0]
    slots = faces + DIRS * halo
    elem_face = elem_face.reshape(-1)
    adjacency = adjacency.reshape(-1)
    halo_list = halo_list.reshape(-1)
    flag = pml_flag.reshape(1, elems)
    tilt = stretch.reshape(1, elems)
    parcels = [(3, ROWS, halo), (2, ROWS, halo), (3, ROWS, halo)]

    def exchange(up, mid, down, sign, beside):
        up = from_behind(up, "gx", 1)
        down = from_behind(down, "gx", -1)
        up, down, beside = lax.optimization_barrier((up, down, beside))
        right, left = call(
            join_kernel, "join", (up, mid, down), [up.shape, up.shape], "aaa" + "vv", [], 2,
            2 * up.shape[0],
        )
        right = from_behind(right, "gy", sign)
        left = from_behind(left, "gy", -sign)
        return (up, down, right, left), beside

    trace_pairs = jnp.transpose(trace_in, (1, 0, 2))
    table, own_sum, *outgoing = call(
        prepare_kernel,
        "prepare",
        (
            trace_pairs, vol_rhs, flag, tilt, jnp.transpose(cond_op, (0, 2, 1, 3)),
            halo_list, elem_face,
        ),
        [(PAD + faces, LANES), (faces, LANES)]
        + [(6, ROWS, halo), (4, ROWS, halo), (6, ROWS, halo)],
        "VVVVVss" + "hhvvv",
        [
            ((PAD + faces, LANES), F32),
            ((LANES, faces), F32),
            ((DIRS * halo, LANES), F32),
            ((faces, LANES), F32),
            ((2 * LANES, elems), F32),
            ((4 * LANES, 2 * LANES), F32),
            ((4, elems, LANES), F32),
        ]
        + [((slots, LANES), F32)] * 8,
        36,
        2,
        15,
    )
    operators = call(
        operators_kernel,
        "operators",
        (
            vol_rhs, flag, tilt, recon_op,
            jnp.transpose(skel_op, (0, 2, 1, 3)), jnp.transpose(lift_op, (0, 3, 1, 2)),
        ),
        [vol_rhs.shape, (blocks * 2 * ROWS, 2 * LANES), (4 * 4 * LANES, 2 * LANES)],
        "VVVVVV" + "VBB",
        [((2 * LANES, elems), F32), ((2 * LANES, 2 * LANES), F32)],
        14,
        0,
        5,
    )
    arrived, operators = exchange(*outgoing, 1, operators)
    recon, skeleton, lifting = operators
    slots_trace, rest = call(
        apply_kernel,
        "apply",
        (table, own_sum, *arrived, skeleton, block_coef, adjacency),
        [(PAD + slots, LANES), (faces, LANES)],
        "hhaaaaBVs" + "hh",
        [
            ((PAD + slots, LANES), F32),
            ((faces, LANES), F32),
            ((faces, LANES), F32),
            ((DIRS, ROWS, halo), F32),
            ((neighbours * TILE, LANES), F32),
            ((neighbours * TILE, LANES), F32),
        ],
        16,
        3 + DIRS,
        16,
    )
    rest_table, *outgoing = call(
        residual_kernel,
        "residual",
        (rest, *arrived, halo_list),
        [(PAD + faces, LANES)] + parcels,
        "haaaas" + "Vvvv",
        [
            ((DIRS, ROWS, halo), F32),
            ((DIRS * halo, LANES), F32),
            ((DIRS, halo, LANES), F32),
        ]
        + [((PAD + faces, LANES), F32)] * 8,
        16,
        1 + DIRS,
        8,
    )
    (base,) = call(
        base_kernel,
        "base",
        (slots_trace, recon, lifting, elem_face),
        [vol_rhs.shape],
        "hVBs" + "V",
        [((PAD + slots, LANES), F32)] + [((4 * LIFT, LANES), F32)] * 2,
        14,
        1,
        8,
    )
    arrived, base = exchange(*outgoing, 1, base)
    (turned,) = call(turn_kernel, "turn", (rest_table,), [(ROWS, faces)], "VV", [], 4)
    across, along = lax.axis_size("gx"), lax.axis_size("gy")
    slots_rest, partial = call(
        image_kernel,
        "image",
        (rest_table, turned, *arrived, skeleton, block_coef, adjacency),
        [(PAD + slots, LANES), (along, LANES)],
        "hVaaaaBVs" + "hv",
        [
            ((PAD + slots, LANES), F32),
            ((DIRS, ROWS, halo), F32),
            ((neighbours * TILE, LANES), F32),
            ((neighbours * TILE, LANES), F32),
        ],
        16,
        3 + DIRS,
        16,
    )
    (lifted,) = call(
        lift_kernel,
        "lift",
        (slots_rest, lifting, elem_face),
        [vol_rhs.shape],
        "hBs" + "V",
        [((PAD + slots, LANES), F32)] + [((4 * LIFT, LANES), F32)] * 2,
        12,
        1,
        7,
    )
    lines, lifted = lax.optimization_barrier((everywhere(partial, "gy"), lifted))
    lines = jnp.sum(lines, axis=0, keepdims=True)
    gathered = everywhere(jnp.broadcast_to(lines, (across, LANES)), "gx")
    trace_pairs, volume_out = call(
        finish_kernel,
        "finish",
        (gathered, trace_pairs, turned, base, lifted),
        [trace_pairs.shape, vol_rhs.shape],
        "vvvvv" + "VV",
        [],
        8,
    )
    trace_out = jnp.transpose(trace_pairs, (1, 0, 2))
    return trace_out, volume_out


def solution(mesh):
    split_last = ("gx", "gy")
    in_specs = (
        P(None, None, split_last),
        P(None, None, split_last),
        P(split_last),
        P(split_last),
        P(),
        P(),
        P(None, None, split_last),
        P(),
        P(),
        P(None, split_last),
        P(None, split_last),
        P(None, split_last),
    )
    out_specs = (P(None, None, split_last), P(None, None, split_last))
    return jax.shard_map(
        local, mesh=mesh, in_specs=in_specs, out_specs=out_specs, check_vma=False
    )
```

```python
import functools

import jax
import jax.numpy as jnp
from jax import lax
from jax.experimental import pallas as pl
from jax.experimental.pallas import tpu as pltpu
from jax.sharding import PartitionSpec as P

F32 = jnp.float32
BF16 = jnp.bfloat16
HALF = 40
ROWS = 2 * HALF
LANES = 128
PAD = 8
DIRS = 8
UNROLL = 128
TILE = 256
LIFT = 256
MIB = 1 << 20


def split(values):
    high = values.astype(BF16)
    return high, (values - high.astype(F32)).astype(BF16)


def dot(left, right, left_dim=1, right_dim=0):
    return lax.dot_general(
        left, right, (((left_dim,), (right_dim,)), ((), ())), preferred_element_type=F32
    )


def half_rolled(block, height):
    wide = jnp.concatenate(
        [block, jnp.zeros((height, LANES - block.shape[1]), F32)], axis=1
    )
    return wide, pltpu.roll(wide, HALF, 1)


def gather_rows(count, indices, source, target, start=0, base=0):
    def some(step, carry):
        first = step * UNROLL
        for extra in range(UNROLL):
            row = indices[start + first + extra]
            target[pl.ds(base + first + extra, 1), :] = source[pl.ds(row + PAD, 1), :]
        return carry

    lax.fori_loop(0, count // UNROLL, some, 0)


def as_stored(table):
    lines, count = table.shape
    return jnp.transpose(table.reshape(lines, count // LANES, LANES), (1, 0, 2)).reshape(-1)


def stored_at(lines, line, entry):
    return (entry // LANES) * (lines * LANES) + line * LANES + entry % LANES


def begin(source, target, semaphore):
    copy = pltpu.make_async_copy(source, target, semaphore)
    copy.start()
    return copy


def parcel_of(rows):
    return rows.T[:ROWS]


def picked_parcel(picked, direction, halo):
    starts = [stored_at(DIRS, direction, first) for first in range(0, halo, LANES)]
    return jnp.concatenate([parcel_of(picked[at : at + LANES, :]) for at in starts], axis=1)


def rows_of(parcel):
    halo = parcel.shape[1]
    return jnp.concatenate([parcel, jnp.zeros((LANES - ROWS, halo), F32)], axis=0).T


def scaled_volume(vol, flag, stretch, scaled):
    nv = vol.shape[1]
    tilt = flag[...].astype(F32) * stretch[...]
    real, imag = vol[0], vol[1]
    fill = jnp.zeros((LANES - nv, vol.shape[2]), F32)
    scaled[0:nv, :] = real - tilt * imag
    scaled[nv:LANES, :] = fill
    scaled[LANES : LANES + nv, :] = imag + tilt * real
    scaled[LANES + nv : 2 * LANES, :] = fill


def place_parcels(picked, halo, lower, middle, upper):
    for direction in range(DIRS):
        parcel = picked_parcel(picked, direction, halo)
        if direction < 3:
            lower[direction] = parcel
        elif direction < 5:
            middle[direction - 3] = parcel
        else:
            upper[direction - 5] = parcel


def prepare_kernel(
    trace, vol, flag, stretch, cond_op, halo_list, elem_face,
    table, own_sum, up, mid, down,
    rows, turned, picked, own, scaled, cond, parts,
    sums0, sums1, sums2, sums3, sums4, sums5, sums6, sums7, done,
):
    nq, faces = trace.shape[0], trace.shape[2]
    nv, elems = vol.shape[1], vol.shape[2]
    halo = up.shape[2]
    turned[...] = jnp.zeros_like(turned)
    turned[0:nq, :] = trace[:, 0, :]
    turned[HALF : HALF + nq, :] = trace[:, 1, :]
    rows[0:PAD, :] = jnp.zeros((PAD, LANES), F32)
    for first in range(0, faces, LANES):
        rows[PAD + first : PAD + first + LANES, :] = turned[:, first : first + LANES].T
    table_copy = begin(rows, table, done.at[0])
    cond[...] = jnp.zeros_like(cond)
    for corner in range(4):
        real, imag = cond_op[corner, :, 0, :], cond_op[corner, :, 1, :]
        low = corner * LANES
        cond[low : low + nq, 0:nv] = real
        cond[low : low + nq, LANES : LANES + nv] = -imag
        cond[low + HALF : low + HALF + nq, 0:nv] = imag
        cond[low + HALF : low + HALF + nq, LANES : LANES + nv] = real
    scaled_volume(vol, flag, stretch, scaled)
    cond_high, cond_rest = split(cond[...])
    for first in range(0, elems, LANES):
        stop = first + LANES
        columns = jnp.concatenate(
            [scaled[0:LANES, first:stop].T, scaled[LANES : 2 * LANES, first:stop].T], axis=1
        )
        high, rest = split(columns)
        product = dot(high, cond_high, 1, 1) + dot(rest, cond_high, 1, 1) + dot(high, cond_rest, 1, 1)
        for corner in range(4):
            parts[corner, first:stop, :] = product[:, corner * LANES : (corner + 1) * LANES]
    sums = (sums0, sums1, sums2, sums3, sums4, sums5, sums6, sums7)
    for total in sums:
        total[...] = jnp.zeros_like(total)
    near = elems // 2

    def add_some(chunk, step, carry):
        first = chunk * 4 * LANES + step * 4
        for extra in range(4):
            elem = chunk * LANES + step * 4 + extra
            places = [
                (corner, elem + part * near) for corner in range(4) for part in range(2)
            ]
            slots = [
                elem_face[first + extra + stored_at(4, corner, part * near)]
                for corner in range(4)
                for part in range(2)
            ]
            before = [total[pl.ds(slot, 1), :] for total, slot in zip(sums, slots)]
            values = [parts[corner, pl.ds(at, 1), :] for corner, at in places]
            for number, total in enumerate(sums):
                total[pl.ds(slots[number], 1), :] = before[number] + values[number]
        return carry

    for chunk in range(near // LANES):
        lax.fori_loop(0, LANES // 4, functools.partial(add_some, chunk), 0)

    def summed(first, size):
        lines = [total[first : first + size, :] for total in sums]
        while len(lines) > 1:
            lines = [lines[k] + lines[k + 1] for k in range(0, len(lines), 2)]
        return lines[0]

    own[...] = summed(0, faces)
    own_copy = begin(own, own_sum, done.at[1])
    gather_rows(DIRS * halo, halo_list, rows, picked)
    for direction in range(DIRS):
        parcel = picked_parcel(picked, direction, halo)
        back = parcel_of(summed(faces + direction * halo, halo))
        if direction < 3:
            down[direction] = parcel
            up[3 + direction] = back
        elif direction < 5:
            mid[direction - 3] = parcel
            mid[direction - 1] = back
        else:
            up[direction - 5] = parcel
            down[direction - 2] = back
    table_copy.wait()
    own_copy.wait()


def halves(real, real_moved, imag, imag_moved, fill):
    high, rest = split(
        jnp.concatenate([real - imag_moved, fill, imag + real_moved, fill], axis=0)
    )
    return jnp.concatenate(
        [
            jnp.concatenate([high, high], axis=1),
            jnp.concatenate([rest, jnp.zeros_like(rest)], axis=1),
        ],
        axis=0,
    )


def operators_kernel(
    vol, flag, stretch, recon_op, skel_op, lift_op, recon_out, skeleton, lifting, scaled, recon
):
    nv, elems = vol.shape[1], vol.shape[2]
    nq = skel_op.shape[1]
    scaled_volume(vol, flag, stretch, scaled)
    for block in range(skel_op.shape[0]):
        low = block * 2 * ROWS
        skeleton[low : low + 2 * ROWS, :] = halves(
            *half_rolled(skel_op[block, :, 0, :], nq),
            *half_rolled(skel_op[block, :, 1, :], nq),
            jnp.zeros((HALF - nq, LANES), F32),
        )
    for corner in range(4):
        low = corner * 4 * LANES
        wide = []
        for part in range(2):
            block = jnp.concatenate(
                [lift_op[corner, :, part, :], jnp.zeros((nq, LANES - nv), F32)], axis=1
            )
            block = jnp.concatenate([block, jnp.zeros((LANES - nq, LANES), F32)], axis=0).T
            wide += [block, pltpu.roll(block, HALF, 1)]
        high, rest = split(jnp.concatenate([wide[0] - wide[3], wide[2] + wide[1]], axis=0))
        lifting[low : low + 2 * LANES, 0:LANES] = high
        lifting[low : low + 2 * LANES, LANES : 2 * LANES] = high
        lifting[low + 2 * LANES : low + 4 * LANES, 0:LANES] = rest
        lifting[low + 2 * LANES : low + 4 * LANES, LANES : 2 * LANES] = jnp.zeros_like(rest)
    recon[...] = jnp.zeros_like(recon)
    recon[0:nv, 0:nv] = recon_op[0]
    recon[0:nv, LANES : LANES + nv] = -recon_op[1]
    recon[LANES : LANES + nv, 0:nv] = recon_op[1]
    recon[LANES : LANES + nv, LANES : LANES + nv] = recon_op[0]
    high, rest = split(recon[...])
    size = 256
    for first in range(0, elems, size):
        stop = first + size
        wanted, fine = split(scaled[:, first:stop])
        product = dot(high, wanted) + dot(high, fine) + dot(rest, wanted)
        recon_out[0, :, first:stop] = product[0:nv]
        recon_out[1, :, first:stop] = product[LANES : LANES + nv]


def skeleton_tile(matrix, block_coef, slots, picked, first, size):
    real_sum = jnp.zeros((HALF, size), F32)
    imag_sum = jnp.zeros((HALF, size), F32)
    for block in range(block_coef.shape[0]):
        if block == 0:
            rows = slots[pl.ds(PAD + first, size), :]
        else:
            rows = picked[(block - 1) * size : block * size, :]
        high, rest = split(rows)
        low = block * 2 * ROWS
        product = dot(
            matrix[low : low + 2 * ROWS, :], jnp.concatenate([high, rest], axis=1), 1, 1
        )
        real = product[0:HALF] + product[ROWS : ROWS + HALF]
        imag = product[HALF:ROWS] + product[ROWS + HALF : 2 * ROWS]
        coef_real = block_coef[block, 0:1, pl.ds(first, size)]
        coef_imag = block_coef[block, 1:2, pl.ds(first, size)]
        real_sum = real_sum + (coef_real * real - coef_imag * imag)
        imag_sum = imag_sum + (coef_real * imag + coef_imag * real)
    return real_sum, imag_sum


def skeleton_loop(matrix, block_coef, adjacency, slots, picked, use, carry):
    tile = TILE
    faces = block_coef.shape[2]
    neighbours = block_coef.shape[0] - 1
    steps = faces // tile

    def fetch(step, target):
        for neighbour in range(neighbours):
            first = neighbour * faces + step * tile
            for extra in range(tile):
                row = adjacency[first + extra]
                at = neighbour * tile + extra
                target[at : at + 1, :] = slots[pl.ds(row + PAD, 1), :]

    def compute(step, source, carry):
        first = pl.multiple_of(step * tile, tile)
        real, imag = skeleton_tile(matrix, block_coef, slots, source, first, tile)
        return use(carry, first, real, imag)

    for neighbour in range(neighbours):
        gather_rows(tile, adjacency, slots, picked[0], neighbour * faces, neighbour * tile)

    def pair(number, carry):
        step = 2 * number
        fetch(step + 1, picked[1])
        carry = compute(step, picked[0], carry)
        fetch(step + 2, picked[0])
        return compute(step + 1, picked[1], carry)

    carry = lax.fori_loop(0, steps // 2 - 1, pair, carry)
    fetch(steps - 1, picked[1])
    carry = compute(steps - 2, picked[0], carry)
    return compute(steps - 1, picked[1], carry)


def join_kernel(up, mid, down, right, left, done):
    moves = [(down, 2, right, 0), (mid, 1, right, 1), (up, 2, right, 2)]
    moves += [(down, 0, left, 0), (mid, 0, left, 1), (up, 0, left, 2)]
    if up.shape[0] == 6:
        moves += [(up, 3, right, 3), (mid, 2, right, 4), (down, 3, right, 5)]
        moves += [(up, 5, left, 3), (mid, 3, left, 4), (down, 5, left, 5)]
    copies = [
        begin(source.at[place], target.at[to], done.at[number])
        for number, (source, place, target, to) in enumerate(moves)
    ]
    for copy in copies:
        copy.wait()


def ghost_places(up, down, right, left):
    return (
        left.at[0], down.at[1], right.at[0], left.at[1],
        right.at[1], left.at[2], up.at[1], right.at[2],
    )


def apply_kernel(
    table, own_sum, up, down, right, left, matrix, block_coef, adjacency,
    slots_out, rest_out,
    slots, own, rest, arrived, picked0, picked1, done,
):
    faces = own.shape[0]
    halo = arrived.shape[2]
    table_copy = begin(table, slots.at[pl.ds(0, PAD + faces)], done.at[0])
    copies = [
        begin(place, arrived.at[direction], done.at[3 + direction])
        for direction, place in enumerate(ghost_places(up, down, right, left))
    ]
    own_copy = begin(own_sum, own, done.at[1])
    for direction in range(DIRS):
        copies[direction].wait()
        first = PAD + faces + direction * halo
        slots[first : first + halo, :] = rows_of(arrived[direction])
    table_copy.wait()
    slots_copy = begin(slots, slots_out, done.at[2])
    own_copy.wait()

    def use(carry, first, real, imag):
        applied = rows_of(jnp.concatenate([real, imag], axis=0))
        rest[pl.ds(first, TILE), :] = own[pl.ds(first, TILE), :] - applied
        return carry

    skeleton_loop(matrix, block_coef, adjacency, slots, (picked0, picked1), use, 0)
    begin(rest, rest_out, done.at[0]).wait()
    slots_copy.wait()


def residual_kernel(
    rest, up, down, right, left, halo_list,
    rest_table, res_up, res_mid, res_down,
    returned, picked, back, sums0, sums1, sums2, sums3, sums4, sums5, sums6, sums7, done,
):
    faces = rest.shape[0]
    halo = returned.shape[2]
    rest_copy = begin(rest, sums0.at[pl.ds(PAD, faces)], done.at[0])
    places = (
        right.at[3], up.at[4], left.at[3], right.at[4],
        left.at[4], right.at[5], down.at[4], left.at[5],
    )
    copies = [
        begin(place, returned.at[direction], done.at[1 + direction])
        for direction, place in enumerate(places)
    ]
    sums0[0:PAD, :] = jnp.zeros((PAD, LANES), F32)
    others = (sums1, sums2, sums3, sums4, sums5, sums6, sums7)
    for total in others:
        total[...] = jnp.zeros_like(total)
    for direction in range(DIRS):
        copies[direction].wait()
        back[direction] = rows_of(returned[direction])
    rest_copy.wait()
    sums = (sums0,) + others

    def add_some(chunk, step, carry):
        first = chunk * DIRS * LANES + step * 4
        for extra in range(4):
            entry = chunk * LANES + step * 4 + extra
            places = [
                halo_list[first + extra + direction * LANES] + PAD for direction in range(DIRS)
            ]
            before = [total[pl.ds(place, 1), :] for total, place in zip(sums, places)]
            values = [back[direction, pl.ds(entry, 1), :] for direction in range(DIRS)]
            for number, total in enumerate(sums):
                total[pl.ds(places[number], 1), :] = before[number] + values[number]
        return carry

    for chunk in range(halo // LANES):
        lax.fori_loop(0, LANES // 4, functools.partial(add_some, chunk), 0)
    rest_table[...] = ((sums0[...] + sums1[...]) + (sums2[...] + sums3[...])) + (
        (sums4[...] + sums5[...]) + (sums6[...] + sums7[...])
    )
    rest_table[0:PAD, :] = jnp.zeros((PAD, LANES), F32)
    gather_rows(DIRS * halo, halo_list, rest_table, picked)
    place_parcels(picked, halo, res_down, res_mid, res_up)


def turn_kernel(rest_table, turned):
    for first in range(0, turned.shape[1], LANES):
        turned[:, first : first + LANES] = parcel_of(
            rest_table[PAD + first : PAD + first + LANES, :]
        )


def lifted_loop(matrix, elem_face, elems, slots, picked, use):
    size = LIFT

    def fetch(step, target):
        for corner in range(4):
            for extra in range(size):
                row = elem_face[stored_at(4, corner, step * size + extra)]
                at = corner * size + extra
                target[at : at + 1, :] = slots[pl.ds(row + PAD, 1), :]

    def compute(step, rows):
        total = jnp.zeros((2 * LANES, size), F32)
        for corner in range(4):
            high, rest = split(rows[corner * size : (corner + 1) * size, :])
            at = corner * 4 * LANES
            product = dot(
                matrix[at : at + 4 * LANES, :], jnp.concatenate([high, rest], axis=1), 1, 1
            )
            total = total + (product[0 : 2 * LANES] + product[2 * LANES : 4 * LANES])
        use(step * size, total)

    steps = elems // size
    fetch(0, picked[0])
    for step in range(steps):
        if step + 1 < steps:
            fetch(step + 1, picked[(step + 1) % 2])
        compute(step, picked[step % 2])


def base_kernel(
    slots_in, recon, matrix, elem_face, base, slots, picked0, picked1, done
):
    nv, elems = base.shape[1], base.shape[2]
    begin(slots_in, slots, done.at[0]).wait()

    def use(first, product):
        stop = first + LIFT
        base[0, :, first:stop] = recon[0, :, first:stop] - product[0:nv]
        base[1, :, first:stop] = recon[1, :, first:stop] - product[LANES : LANES + nv]

    lifted_loop(matrix, elem_face, elems, slots, (picked0, picked1), use)


def lift_kernel(slots_in, matrix, elem_face, lifted, slots, picked0, picked1, done):
    nv, elems = lifted.shape[1], lifted.shape[2]
    begin(slots_in, slots, done.at[0]).wait()

    def use(first, product):
        stop = first + LIFT
        lifted[0, :, first:stop] = product[0:nv]
        lifted[1, :, first:stop] = product[LANES : LANES + nv]

    lifted_loop(matrix, elem_face, elems, slots, (picked0, picked1), use)


def image_kernel(
    rest_table, turned, up, down, right, left, matrix, block_coef, adjacency,
    slots_out, partial,
    slots, arrived, picked0, picked1, done,
):
    faces = turned.shape[1]
    halo = arrived.shape[2]
    table_copy = begin(rest_table, slots.at[pl.ds(0, PAD + faces)], done.at[0])
    copies = [
        begin(place, arrived.at[direction], done.at[3 + direction])
        for direction, place in enumerate(ghost_places(up, down, right, left))
    ]
    for direction in range(DIRS):
        copies[direction].wait()
        first = PAD + faces + direction * halo
        slots[first : first + halo, :] = rows_of(arrived[direction])
    table_copy.wait()
    slots_copy = begin(slots, slots_out, done.at[2])

    def use(carry, first, real, imag):
        rest_real = turned[0:HALF, pl.ds(first, TILE)]
        rest_imag = turned[HALF:ROWS, pl.ds(first, TILE)]
        return (
            carry[0] + (real * rest_real + imag * rest_imag),
            carry[1] + (real * rest_imag - imag * rest_real),
            carry[2] + (real * real + imag * imag),
        )

    zero = jnp.zeros((HALF, TILE), F32)
    totals = skeleton_loop(
        matrix, block_coef, adjacency, slots, (picked0, picked1), use, (zero, zero, zero)
    )
    lane = lax.broadcasted_iota(jnp.int32, (1, LANES), 1)
    line = jnp.zeros((1, LANES), F32)
    for place in range(3):
        line = line + jnp.where(lane == place, jnp.sum(totals[place]), 0.0)
    partial[...] = jnp.broadcast_to(line, partial.shape)
    slots_copy.wait()


def finish_kernel(gathered, trace, turned, base, lifted, trace_out, volume_out):
    nq = trace.shape[0]
    line = jnp.sum(gathered[...], axis=0, keepdims=True)
    lane = lax.broadcasted_iota(jnp.int32, (1, LANES), 1)
    entry = [
        jnp.sum(jnp.where(lane == place, line, 0.0), axis=1, keepdims=True)
        for place in range(3)
    ]
    step_real = entry[0] / entry[2]
    step_imag = entry[1] / entry[2]
    volume_out[0] = base[0] - (step_real * lifted[0] - step_imag * lifted[1])
    volume_out[1] = base[1] - (step_real * lifted[1] + step_imag * lifted[0])
    rest_real = turned[0:nq, :]
    rest_imag = turned[HALF : HALF + nq, :]
    trace_out[:, 0, :] = trace[:, 0, :] + (step_real * rest_real - step_imag * rest_imag)
    trace_out[:, 1, :] = trace[:, 1, :] + (step_real * rest_imag + step_imag * rest_real)


SPACES = {
    "v": pltpu.MemorySpace.VMEM,
    "s": pltpu.MemorySpace.SMEM,
    "a": pl.ANY,
    "h": pltpu.HBM,
    "V": pltpu.MemorySpace.VMEM,
    "B": pltpu.MemorySpace.VMEM,
    "S": pltpu.MemorySpace.SMEM,
}


def call(kernel, name, args, out_shapes, spaces, scratch, limit, semaphores=0, time=1):
    specs = [pl.BlockSpec(memory_space=SPACES[letter]) for letter in spaces]
    shapes = [pltpu.VMEM(shape, kind) for shape, kind in scratch]
    if semaphores:
        shapes.append(pltpu.SemaphoreType.DMA((semaphores,)))
    args = [
        pltpu.with_memory_space_constraint(arg, pltpu.HBM) if letter in "hVBS" else arg
        for arg, letter in zip(args, spaces)
    ]
    return pl.pallas_call(
        kernel,
        name=name,
        out_shape=[
            pltpu.HBM(shape, BF16 if letter == "B" else F32)
            if letter in "hVB"
            else jax.ShapeDtypeStruct(shape, F32)
            for shape, letter in zip(out_shapes, spaces[len(args) :])
        ],
        in_specs=specs[: len(args)],
        out_specs=specs[len(args) :],
        scratch_shapes=shapes,
        compiler_params=pltpu.CompilerParams(vmem_limit_bytes=limit * MIB),
        cost_estimate=pl.CostEstimate(
            flops=0, bytes_accessed=3300000 * time, transcendentals=0
        ),
    )(*args)


def from_behind(block, axis, distance):
    devices = range(lax.axis_size(axis))
    route = [(i - distance, i) for i in devices if i - distance in devices]
    return lax.ppermute(block, axis, route)


def everywhere(lines, axis):
    return lax.all_to_all(lines, axis, 0, 0)


def local(
    vol_rhs, trace_in, pml_flag, stretch, cond_op, skel_op, block_coef, recon_op, lift_op,
    elem_face, adjacency, halo_list,
):
    nv, elems = vol_rhs.shape[1], vol_rhs.shape[2]
    faces = trace_in.shape[2]
    halo = halo_list.shape[1]
    blocks = skel_op.shape[0]
    neighbours = adjacency.shape[0]
    slots = faces + DIRS * halo
    elem_face = as_stored(elem_face)
    adjacency = adjacency.reshape(-1)
    halo_list = as_stored(halo_list)
    flag = pml_flag.reshape(1, elems)
    tilt = stretch.reshape(1, elems)
    parcels = [(3, ROWS, halo), (2, ROWS, halo), (3, ROWS, halo)]

    def exchange(up, mid, down, sign, beside):
        up = from_behind(up, "gx", 1)
        down = from_behind(down, "gx", -1)
        up, down, beside = lax.optimization_barrier((up, down, beside))
        right, left = call(
            join_kernel, "join", (up, mid, down), [up.shape, up.shape], "aaa" + "vv", [], 2,
            2 * up.shape[0],
        )
        right = from_behind(right, "gy", sign)
        left = from_behind(left, "gy", -sign)
        return (up, down, right, left), beside

    trace_pairs = jnp.transpose(trace_in, (1, 0, 2))
    table, own_sum, *outgoing = call(
        prepare_kernel,
        "prepare",
        (
            trace_pairs, vol_rhs, flag, tilt, jnp.transpose(cond_op, (0, 2, 1, 3)),
            halo_list, elem_face,
        ),
        [(PAD + faces, LANES), (faces, LANES)]
        + [(6, ROWS, halo), (4, ROWS, halo), (6, ROWS, halo)],
        "VVVVVSS" + "hhvvv",
        [
            ((PAD + faces, LANES), F32),
            ((LANES, faces), F32),
            ((DIRS * halo, LANES), F32),
            ((faces, LANES), F32),
            ((2 * LANES, elems), F32),
            ((4 * LANES, 2 * LANES), F32),
            ((4, elems, LANES), F32),
        ]
        + [((slots, LANES), F32)] * 8,
        36,
        2,
        15,
    )
    operators = call(
        operators_kernel,
        "operators",
        (
            vol_rhs, flag, tilt, recon_op,
            jnp.transpose(skel_op, (0, 2, 1, 3)), jnp.transpose(lift_op, (0, 3, 1, 2)),
        ),
        [vol_rhs.shape, (blocks * 2 * ROWS, 2 * LANES), (4 * 4 * LANES, 2 * LANES)],
        "VVVVVV" + "VBB",
        [((2 * LANES, elems), F32), ((2 * LANES, 2 * LANES), F32)],
        14,
        0,
        5,
    )
    arrived, operators = exchange(*outgoing, 1, operators)
    recon, skeleton, lifting = operators
    slots_trace, rest = call(
        apply_kernel,
        "apply",
        (table, own_sum, *arrived, skeleton, block_coef, adjacency),
        [(PAD + slots, LANES), (faces, LANES)],
        "hhaaaaBVs" + "hh",
        [
            ((PAD + slots, LANES), F32),
            ((faces, LANES), F32),
            ((faces, LANES), F32),
            ((DIRS, ROWS, halo), F32),
            ((neighbours * TILE, LANES), F32),
            ((neighbours * TILE, LANES), F32),
        ],
        16,
        3 + DIRS,
        16,
    )
    rest_table, *outgoing = call(
        residual_kernel,
        "residual",
        (rest, *arrived, halo_list),
        [(PAD + faces, LANES)] + parcels,
        "haaaas" + "Vvvv",
        [
            ((DIRS, ROWS, halo), F32),
            ((DIRS * halo, LANES), F32),
            ((DIRS, halo, LANES), F32),
        ]
        + [((PAD + faces, LANES), F32)] * 8,
        16,
        1 + DIRS,
        8,
    )
    (base,) = call(
        base_kernel,
        "base",
        (slots_trace, recon, lifting, elem_face),
        [vol_rhs.shape],
        "hVBs" + "V",
        [((PAD + slots, LANES), F32)] + [((4 * LIFT, LANES), F32)] * 2,
        14,
        1,
        8,
    )
    arrived, base = exchange(*outgoing, 1, base)
    (turned,) = call(turn_kernel, "turn", (rest_table,), [(ROWS, faces)], "VV", [], 4)
    across, along = lax.axis_size("gx"), lax.axis_size("gy")
    slots_rest, partial = call(
        image_kernel,
        "image",
        (rest_table, turned, *arrived, skeleton, block_coef, adjacency),
        [(PAD + slots, LANES), (along, LANES)],
        "hVaaaaBVs" + "hv",
        [
            ((PAD + slots, LANES), F32),
            ((DIRS, ROWS, halo), F32),
            ((neighbours * TILE, LANES), F32),
            ((neighbours * TILE, LANES), F32),
        ],
        16,
        3 + DIRS,
        16,
    )
    (lifted,) = call(
        lift_kernel,
        "lift",
        (slots_rest, lifting, elem_face),
        [vol_rhs.shape],
        "hBs" + "V",
        [((PAD + slots, LANES), F32)] + [((4 * LIFT, LANES), F32)] * 2,
        12,
        1,
        7,
    )
    lines, lifted = lax.optimization_barrier((everywhere(partial, "gy"), lifted))
    lines = jnp.sum(lines, axis=0, keepdims=True)
    gathered = everywhere(jnp.broadcast_to(lines, (across, LANES)), "gx")
    trace_pairs, volume_out = call(
        finish_kernel,
        "finish",
        (gathered, trace_pairs, turned, base, lifted),
        [trace_pairs.shape, vol_rhs.shape],
        "vvvvv" + "VV",
        [],
        8,
    )
    trace_out = jnp.transpose(trace_pairs, (1, 0, 2))
    return trace_out, volume_out


def solution(mesh):
    split_last = ("gx", "gy")
    in_specs = (
        P(None, None, split_last),
        P(None, None, split_last),
        P(split_last),
        P(split_last),
        P(),
        P(),
        P(None, None, split_last),
        P(),
        P(),
        P(None, split_last),
        P(None, split_last),
        P(None, split_last),
    )
    out_specs = (P(None, None, split_last), P(None, None, split_last))
    return jax.shard_map(
        local, mesh=mesh, in_specs=in_specs, out_specs=out_specs, check_vma=False
    )
```
